256 devices in a mesh: inst: 8 (over y, z_hi), cell: 32 (over x, z_lo, core).
Axes of the slice: x: 4, y: 4, z: 8 (z_hi: 2, z_lo: 4; z = z_hi * 4 + z_lo), core: 2. Of those that a mesh axis runs over, the one named last changes fastest.
Arguments:
- adjoint: bfloat16 [16, 5, 64, 64, 256], P('inst', None, 'cell'), may hold values from -6 to 6
- flux_jac: bfloat16 [16, 5, 3, 64, 64, 256], P('inst', None, None, 'cell'), may hold values from -0.625 to 0.625
- shift: float32 [64, 64, 256], P('cell', 'inst'), may hold values from 0.1 to 2
Outputs:
- mesh_adjoint: float32 [3, 64, 64, 256], P(None, 'cell', 'inst')
- residual: float32 [3, 64, 64, 256], P(None, 'cell', 'inst')
The draws below stay inside these ranges and needn't reach their ends.
All inputs are finite; a program needn't handle non-finite values.
Results may differ from the reference program's by a relative error of at most 0.0003.
Values may be sent and summed in bfloat16 or wider, within the bound.
No kernel may reach another device: no remote copies, remote signals or barrier semaphores. Data moves between devices by JAX's collectives and lax.ppermute only.
A program may use at most 64 MiB of HBM per device.

```python
import math
import jax
import jax.numpy as jnp
from jax import lax

NV = 5
NC = 3
ITERS = 3
NZ = 256
INSTANCES = 16
NX = 64
NY = 64


def strengthened(entries, key, source, target, parts, factor):
    owner, partner = [(jnp.arange(entries.shape[axis_at]) // (entries.shape[axis_at] // parts)).reshape([-1 if axis == axis_at else 1 for axis in range(entries.ndim)]) for axis_at in (source, target)]
    chosen = jax.random.permutation(key, parts)[partner]
    strong = (owner == chosen) | (owner == (partner + parts // 2) % parts)
    return jnp.where(strong, factor * entries, entries)


def steps_of(key, extent, cuts, low, top_value):
    gain = 1.0
    for axis_at, blocks in cuts:
        steps = jax.random.uniform(jax.random.fold_in(jax.random.fold_in(key, 6), axis_at), (blocks,), jnp.float32, low / len(cuts), top_value / len(cuts))
        gain = gain * jnp.repeat(jnp.exp(steps), extent[axis_at] // blocks).reshape((-1,) + (1,) * (len(extent) - 1 - axis_at))
    return gain


def bell_draw(key, shape, spread, reach, split=(), kind=jnp.bfloat16):
    drawn = jax.random.normal(key, shape, jnp.float32) * spread
    if len(split) > 0:
        drawn = steps_of(key, shape, split, -0.22, 0.18) * drawn
    return jnp.clip(drawn, min=-reach, max=reach).astype(kind)


def heavy_noise(rng, extent, spread, reach, split, heavy, dtype=jnp.bfloat16):
    array = spread * jax.random.normal(rng, extent, jnp.float32)
    if split:
        array = array * steps_of(rng, extent, split, -0.22, 0.18)
    return jnp.clip(strengthened(array, jax.random.fold_in(rng, 3), *heavy), -reach, reach).astype(dtype)


def setup_inputs(seed: int = 0) -> dict:
    splits = jax.random.split(jax.random.key(seed), 4)
    return {
        "adjoint": bell_draw(splits[0], (INSTANCES, NV, NX, NY, NZ), 1.0, 6.0, ((0, 8), (2, 32))),
        "flux_jac": heavy_noise(splits[1], (INSTANCES, NV, NC, NX, NY, NZ), (2 * NV * INSTANCES) ** -0.5, 0.625, ((0, 8), (3, 32)), (0, 4, 8, 2.0)),
        "shift": jnp.clip(jnp.exp(math.log(2.0) - 2.9957323 * jax.random.uniform(splits[2], (NX, NY, NZ), jnp.float32) ** steps_of(splits[2], (NX, NY, NZ), ((0, 32), (1, 8)), -0.2, 0.2)), 0.1, 2.0),
    }


mu_shear = 1.0
lame_first = 1.5


def instance_term(total, pair):
    adjoint_one, flux_one = pair
    padded = jnp.pad(adjoint_one.astype(jnp.float32), ((0, 0), (1, 1), (0, 0), (0, 0)))
    flux_full = flux_one.astype(jnp.float32)
    upper = jnp.einsum("vkxyz,vxyz->kxyz", flux_full, padded[:, 2:], precision=lax.Precision.HIGHEST)
    lower = jnp.einsum("vkxyz,vxyz->kxyz", flux_full, padded[:, :-2], precision=lax.Precision.HIGHEST)
    return total + (upper - lower), None


def operate(field, shift):
    padded = jnp.pad(field, ((0, 0), (1, 1), (1, 1), (1, 1)))
    beside = padded[:, 2:, 1:-1, 1:-1] + padded[:, :-2, 1:-1, 1:-1]
    beside = beside + padded[:, 1:-1, 2:, 1:-1] + padded[:, 1:-1, :-2, 1:-1]
    beside = beside + padded[:, 1:-1, 1:-1, 2:] + padded[:, 1:-1, 1:-1, :-2]
    diverge = (padded[0, 2:, 1:-1, 1:-1] - field[0]) + (padded[1, 1:-1, 2:, 1:-1] - field[1]) + (padded[2, 1:-1, 1:-1, 2:] - field[2])
    low_pad = jnp.pad(diverge, ((1, 0), (1, 0), (1, 0)))
    grad_part = jnp.stack([low_pad[:-1, 1:, 1:] - diverge, low_pad[1:, :-1, 1:] - diverge, low_pad[1:, 1:, :-1] - diverge])
    return mu_shear * (6.0 * field - beside) + shift * field + lame_first * grad_part


def reference(adjoint, flux_jac, shift):
    start = jnp.zeros((NC, NX, NY, NZ), jnp.float32)
    sens, _ = lax.scan(instance_term, start, (adjoint, flux_jac))
    mesh_adjoint = jnp.zeros_like(sens)
    residual, direction = sens, sens
    norm_now = jnp.sum(residual * residual)
    for sweep in range(ITERS):
        image = operate(direction, shift)
        alpha = norm_now / jnp.sum(direction * image)
        mesh_adjoint = mesh_adjoint + alpha * direction
        residual = residual - alpha * image
        norm_next = jnp.sum(residual * residual)
        direction = residual + (norm_next / norm_now) * direction
        norm_now = norm_next
    return mesh_adjoint, residual
```

```python
import jax
import jax.numpy as jnp
import numpy as np
from jax import lax
from jax.sharding import PartitionSpec as P

ITERS = 3
MU = 1.0
LAME = 1.5
NYC, NZH, NXC, NZL, NCORE = 4, 2, 4, 4, 2
BOTH = ("inst", "cell")


def flat(y, zh, x, zl, core):
    return (((y * NZH + zh) * NXC + x) * NZL + zl) * NCORE + core


def perm_of(move):
    pairs = []
    for y, zh, x, zl, core in np.ndindex(NYC, NZH, NXC, NZL, NCORE):
        pairs.append((flat(y, zh, x, zl, core), flat(*move(y, zh, x, zl, core))))
    return pairs


def send_core(v):
    return lax.ppermute(v, "cell", [(c, c ^ 1) for c in range(32)])


def send_x(v, d):
    return lax.ppermute(v, "cell", [(c, (c + 8 * d) % 32) for c in range(32)])


def send_y(v, d):
    return lax.ppermute(v, "inst", [(i, (i + 2 * d) % 8) for i in range(8)])


def send_zh(v):
    return lax.ppermute(v, "inst", [(i, i ^ 1) for i in range(8)])


def send_z(v, d):
    def move(y, zh, x, zl, core):
        z = (zh * NZL + zl + d) % (NZH * NZL)
        return y, z // NZL, x, z % NZL, core

    return lax.ppermute(v, BOTH, perm_of(move))


def send_cell(v, d):
    return lax.ppermute(v, "cell", [(c, c + d) for c in range(32) if 0 <= c + d < 32])


def send_inst(v, d):
    return lax.ppermute(v, "inst", [(i, i + d) for i in range(8) if 0 <= i + d < 8])


def all_sum(v):
    v = v + send_core(v)
    v = v + send_y(v, 1) + send_y(v, -1) + send_y(v, 2)
    v = v + send_x(v, 1) + send_x(v, -1) + send_x(v, 2)
    low, high = send_z(v, 1), send_z(v, -1)
    pair = low + v
    triple = pair + high
    return triple + send_z(triple, 3) + send_z(pair, -3)


def operate(u, shift, x0, y0, rows, cols):
    p = jnp.pad(u, ((0, 0), (0, 0), (0, 0), (1, 1)))
    center = p[:, 1:-1, 1:-1, 1:-1]
    beside = p[:, 2:, 1:-1, 1:-1] + p[:, :-2, 1:-1, 1:-1]
    beside = beside + p[:, 1:-1, 2:, 1:-1] + p[:, 1:-1, :-2, 1:-1]
    beside = beside + p[:, 1:-1, 1:-1, 2:] + p[:, 1:-1, 1:-1, :-2]
    corner = p[:, :-1, :-1, :-1]
    dv = (
        (p[0, 1:, :-1, :-1] - corner[0])
        + (p[1, :-1, 1:, :-1] - corner[1])
        + (p[2, :-1, :-1, 1:] - corner[2])
    )
    nx, ny, nz = dv.shape
    gx = x0 + jnp.arange(nx)
    gy = y0 + jnp.arange(ny)
    gz = jnp.arange(nz) - 1
    inside_x = (gx >= 0) & (gx < rows)
    inside_y = (gy >= 0) & (gy < cols)
    inside = inside_x[:, None, None] & inside_y[None, :, None]
    dv = jnp.where(inside & (gz >= 0)[None, None, :], dv, 0.0)
    inner = dv[1:, 1:, 1:]
    grad = jnp.stack([dv[:-1, 1:, 1:] - inner, dv[1:, :-1, 1:] - inner, dv[1:, 1:, :-1] - inner])
    image = MU * (6.0 * center - beside) + shift * center + LAME * grad
    return jnp.where(inside[1:, 1:], image, 0.0)


def cg_coefficients(m):
    zero = jnp.zeros_like(m[0])
    one = zero + 1.0

    def dot(u, v):
        return sum(u[i] * v[j] * m[i + j] for i in range(4) for j in range(4) if i + j < 6)

    r, p, x = [one, zero, zero, zero], [one, zero, zero, zero], [zero] * 4
    now = m[0]
    for sweep in range(ITERS):
        q = [zero] + p[:3]
        alpha = now / dot(p, q)
        x = [a + alpha * b for a, b in zip(x, p)]
        r = [a - alpha * b for a, b in zip(r, q)]
        if sweep < ITERS - 1:
            new = dot(r, r)
            p = [a + new / now * b for a, b in zip(r, p)]
            now = new
    return x[:3], r


def local(adjoint, flux_jac, shift):
    nx, ny, nz = shift.shape
    cell = lax.axis_index("cell")
    inst = lax.axis_index("inst")
    y, zh = inst // 2, inst % 2
    rows, cols = nx * 32, ny * 8

    low = send_cell(adjoint[:, :, -1:], 1)
    high = send_cell(adjoint[:, :, :1], -1)
    padded = jnp.concatenate([low, adjoint, high], axis=2).astype(jnp.float32)
    step = padded[:, :, 2:] - padded[:, :, :-2]
    part = jnp.sum(flux_jac.astype(jnp.float32) * step[:, :, None], axis=(0, 1))

    sy = jnp.concatenate([send_inst(shift[:, -2:], 1), shift, send_inst(shift[:, :2], -1)], axis=1)
    shift_ext = jnp.concatenate([send_cell(sy, 1), sy, send_cell(sy, -1)], axis=0)

    wide = jnp.pad(part, ((0, 0), (0, 0), (3, 3), (0, 0)))

    def chunk(d):
        return lax.dynamic_slice_in_dim(wide, 2 * ny * ((y + d) % 4), 2 * ny + 6, 2)

    total = chunk(0)
    for d in (2, 1, 3):
        total = total + send_y(chunk(d), d)
    mine = lax.dynamic_slice_in_dim(total, ny * zh, ny + 6, 2)
    other = lax.dynamic_slice_in_dim(total, ny * (1 - zh), ny + 6, 2)
    block = mine + send_zh(other)
    field = jnp.concatenate(
        [send_cell(block[:, 1:], 2), send_cell(block, 1), block, send_cell(block, -1), send_cell(block[:, :1], -2)],
        axis=1,
    )
    x0, y0 = cell * nx - 3, inst * ny - 3
    w0 = field
    w1 = operate(w0, shift_ext, x0, y0, rows, cols)
    w2 = operate(w1, shift_ext[1:-1, 1:-1], x0 + 1, y0 + 1, rows, cols)
    w3 = operate(w2, shift, x0 + 2, y0 + 2, rows, cols)
    w = [w0[:, 3:-3, 3:-3], w1[:, 2:-2, 2:-2], w2[:, 1:-1, 1:-1], w3]
    pairs = ((0, 0), (0, 1), (1, 1), (1, 2), (2, 2), (2, 3))
    lanes = jnp.stack([jnp.sum((w[i] * w[j]).reshape(-1, 128), axis=0) for i, j in pairs])
    moments = jnp.sum(all_sum(lanes), axis=1)
    cx, cr = cg_coefficients([moments[k] for k in range(6)])
    mesh_adjoint = cx[0] * w[0] + cx[1] * w[1] + cx[2] * w[2]
    residual = cr[0] * w[0] + cr[1] * w[1] + cr[2] * w[2] + cr[3] * w[3]
    return mesh_adjoint, residual


def solution(mesh):
    placed = (
        P("inst", None, "cell", None, None),
        P("inst", None, None, "cell", None, None),
        P("cell", "inst", None),
    )
    return jax.shard_map(
        local,
        mesh=mesh,
        in_specs=placed,
        out_specs=(P(None, "cell", "inst", None), P(None, "cell", "inst", None)),
        check_vma=False,
    )
```

```python
import jax
import jax.numpy as jnp
import numpy as np
from jax import lax
from jax.experimental import pallas as pl
from jax.experimental.pallas import tpu as pltpu
from jax.sharding import Mesh, PartitionSpec as P

ITERS = 3
MU = 1.0
LAME = 1.5
AXES = ("y", "zh", "x", "zl", "core")
SIZES = (4, 2, 4, 4, 2)
F32 = jnp.float32


def flat(at):
    index = 0
    for size, k in zip(SIZES, at):
        index = index * size + k
    return index


def send(v, move):
    pairs = []
    for at in np.ndindex(*SIZES):
        to = move(*at)
        if to is not None:
            pairs.append((flat(at), flat(to)))
    return lax.ppermute(v, AXES, pairs)


def send_y(v, d):
    return send(v, lambda y, zh, x, zl, core: ((y + d) % 4, zh, x, zl, core))


def send_zh(v):
    return send(v, lambda y, zh, x, zl, core: (y, 1 - zh, x, zl, core))


def send_core(v):
    return send(v, lambda y, zh, x, zl, core: (y, zh, x, zl, 1 - core))


def send_cell(v, d):
    def move(y, zh, x, zl, core):
        c = x * 8 + zl * 2 + core + d
        return (y, zh, c // 8, c // 2 % 4, c % 2) if 0 <= c < 32 else None

    return send(v, move)


def send_chip(v, low_core):
    def move(y, zh, x, zl, core):
        q = x * 4 + zl + (low_core if core == 0 else -low_core)
        return (y, zh, q // 4, q % 4, core) if 0 <= q < 16 else None

    return send(v, move)


VMEM = pl.BlockSpec(memory_space=pltpu.VMEM)
SMEM = pl.BlockSpec(memory_space=pltpu.SMEM)


def call(kernel, outs, args, scratch=()):
    return pl.pallas_call(
        kernel,
        out_shape=[jax.ShapeDtypeStruct(s, F32) for s in outs],
        in_specs=[SMEM] + [VMEM] * (len(args) - 1),
        out_specs=[VMEM] * len(outs),
        scratch_shapes=list(scratch),
        compiler_params=pltpu.CompilerParams(vmem_limit_bytes=24 * 1024 * 1024),
    )(*args)


def sens_kernel(pos, f, a, lo, hi, shift, m0, m1, m2, m3, wide):
    y = pos[0]
    zero = jnp.zeros((8, 256), F32)
    for s in range(6):
        wide[s, 0:8, :] = zero
        wide[s, 64:72, :] = zero
    for rows in range(0, 64, 16):
        span = slice(rows, rows + 16)
        for x in range(2):
            total = [None] * 3
            for i in range(2):
                for v in range(5):
                    if x == 0:
                        up, down = a[i, v, 1, span, :], lo[i, v, 0, span, :]
                    else:
                        up, down = hi[i, v, 0, span, :], a[i, v, 0, span, :]
                    step = up.astype(F32) - down.astype(F32)
                    for k in range(3):
                        term = f[i, v, k, x, span, :].astype(F32) * step
                        total[k] = term if total[k] is None else total[k] + term
            for k in range(3):
                wide[k * 2 + x, rows + 3 : rows + 19, :] = total[k]
    for d, out in ((0, m0), (1, m1), (2, m2), (3, m3)):
        first = pl.multiple_of(lax.rem(y + d, 4) * 16, 16)
        for s in range(6):
            out[s * 3 : s * 3 + 3] = wide[s, pl.ds(first, 24), :].reshape(3, 8, 256)
    for out in (m1, m3):
        out[18:20] = shift[...]


def sum_y_kernel(pos, m0, r1, r2, r3, shift, own, out):
    zh = pos[1]
    for s in range(6):
        for g in range(2):
            for half, to in ((zh, own), (1 - zh, out)):
                k = s * 3 + half + g
                to[s * 2 + g] = (m0[k] + r1[k]) + (r2[k] + r3[k])
    low = zh == 0
    for x in range(2):
        below = jnp.where(low, shift[x, 6:8, :], r1[18 + x, 6:8, :])
        above = jnp.where(low, r3[18 + x, 0:2, :], shift[x, 0:2, :])
        out[12, x * 4 : x * 4 + 2, :] = below
        out[12, x * 4 + 2 : x * 4 + 4, :] = above


def block_kernel(pos, own, got, shift, block):
    for s in range(6):
        for g in range(2):
            block[s // 2, s % 2, g * 8 : g * 8 + 8, :] = own[s * 2 + g] + got[s * 2 + g]
    for x in range(2):
        block[3, x, 0:8, :] = jnp.zeros((8, 256), F32)
        block[3, x, 8:16, :] = jnp.zeros((8, 256), F32)
        block[3, x, 3:11, :] = shift[x]
        block[3, x, 1:3, :] = got[12, x * 4 : x * 4 + 2, :]
        block[3, x, 11:13, :] = got[12, x * 4 + 2 : x * 4 + 4, :]


def krylov_kernel(pos, own, mate, far, near, basis, moments, w1, w2):
    inst, cell, core = pos[2], pos[3], pos[4]
    even = core == 0

    def pick(p, q):
        return jnp.where(even, p, q)

    def start(k, x):
        if x in (3, 4):
            return own[k, x - 3]
        if x in (0, 7):
            return pick(far[k * 3], near[k]) if x == 0 else pick(near[k], far[k * 3 + 2])
        if x in (1, 2):
            return pick(far[k * 3 + x], mate[k, x - 1])
        return pick(mate[k, x - 5], far[k * 3 + x - 5])

    def shift_at(x):
        if x in (3, 4):
            return own[3, x - 3]
        if x in (1, 2):
            return pick(far[9 + x - 1], mate[3, x - 1])
        return pick(mate[3, x - 5], far[9 + x - 5])

    row = lax.broadcasted_iota(jnp.int32, (16, 256), 0) + (inst * 8 - 3)
    lane = lax.broadcasted_iota(jnp.int32, (16, 256), 1)
    in_row = (row >= 0) & (row < 64)
    first, last = lane == 0, lane == 255

    def inside(x):
        at = cell * 2 - 3 + x
        return in_row & jnp.broadcast_to((at >= 0) & (at < 64), (16, 256))

    def y_up(v):
        return pltpu.roll(v, 15, 0)

    def y_down(v):
        return pltpu.roll(v, 1, 0)

    def z_up(v):
        return jnp.where(last, 0.0, pltpu.roll(v, 255, 1))

    def z_down(v):
        return jnp.where(first, 0.0, pltpu.roll(v, 1, 1))

    def apply(u, lo, hi, keep):
        before = None
        for x in range(lo - 1, hi + 1):
            c = [u(k, x) for k in range(3)]
            u1y, u2z = y_up(c[1]), z_up(c[2])
            dv = (u(0, x + 1) - c[0]) + (u1y - c[1]) + (u2z - c[2])
            mask = inside(x)
            dv = jnp.where(mask, dv, 0.0)
            if x >= lo:
                ups = [(y_up(c[0]), z_up(c[0])), (u1y, z_up(c[1])), (y_up(c[2]), u2z)]
                grads = [before, y_down(dv), z_down(dv)]
                weight = shift_at(x) + 6.0 * MU
                for k in range(3):
                    beside = (u(k, x + 1) + u(k, x - 1)) + (ups[k][0] + y_down(c[k]))
                    beside = beside + (ups[k][1] + z_down(c[k]))
                    image = weight * c[k] - MU * beside + LAME * (grads[k] - dv)
                    keep(k, x, jnp.where(mask, image, 0.0))
            before = dv

    def put(ref):
        def keep(k, x, v):
            ref[k, x] = v

        return keep

    apply(start, 1, 6, put(w1))
    apply(lambda k, x: w1[k, x], 2, 5, put(w2))
    sums = [None] * 6

    def finish(k, x, v):
        w = [own[k, x - 3, 3:11, :], w1[k, x, 3:11, :], w2[k, x, 3:11, :], v[3:11, :]]
        for j in range(4):
            basis[j, k, x - 3] = w[j]
        for n, (i, j) in enumerate(((0, 0), (0, 1), (1, 1), (1, 2), (2, 2), (2, 3))):
            term = w[i] * w[j]
            sums[n] = term if sums[n] is None else sums[n] + term

    apply(lambda k, x: w2[k, x], 3, 4, finish)
    moments[...] = jnp.zeros((8, 128), F32)
    for n in range(6):
        line = jnp.sum(sums[n], axis=0, keepdims=True)
        moments[n : n + 1, :] = line[:, :128] + line[:, 128:]


def two_sum(a, b):
    s = a + b
    t = s - a
    return s, (a - (s - t)) + (b - t)


def two_product(a, b):
    def halves(v):
        t = 4097.0 * v
        high = t - (t - v)
        return high, v - high

    p = a * b
    ah, al = halves(a)
    bh, bl = halves(b)
    return p, ((ah * bh - p) + ah * bl + al * bh) + al * bl


def finish_kernel(pos, parts, basis, mesh_adjoint, residual):
    high = parts[0]
    low = jnp.zeros((8, 128), F32)
    for n in range(1, parts.shape[0]):
        high, error = two_sum(high, parts[n])
        low = low + error
    for step in (64, 32, 16, 8, 4, 2, 1):
        high, error = two_sum(high, pltpu.roll(high, step, 1))
        low = (low + pltpu.roll(low, step, 1)) + error

    def line(v, n):
        return jnp.broadcast_to(v[n : n + 1, :], (8, 128))

    t = line(high, 1) / line(high, 0)
    centred = [line(high, 0) + line(low, 0)]
    for n in range(1, 6):
        product, error = two_product(t, high)
        error = error + t * low
        high, more = two_sum(pltpu.roll(high, 7, 0), -product)
        low = (pltpu.roll(low, 7, 0) - error) + more
        high, low = two_sum(high, low)
        centred.append(line(high, 0) + line(low, 0))

    def dot(u, v):
        total = None
        for i, p in enumerate(u):
            for j, q in enumerate(v):
                term = p * q * centred[i + j]
                total = term if total is None else total + term
        return total

    one = jnp.ones((8, 128), F32)
    r, p, x, now = [one], [one], [], centred[0]
    for sweep in range(ITERS):
        image = [t * p[0]] + [p[n - 1] + t * p[n] for n in range(1, len(p))] + [p[-1]]
        alpha = now / dot(p, image)
        x = [x[n] + alpha * p[n] if n < len(x) else alpha * p[n] for n in range(len(p))]
        r = [r[n] - alpha * image[n] if n < len(r) else -alpha * image[n] for n in range(len(image))]
        if sweep < ITERS - 1:
            new = dot(r, r)
            beta = new / now
            p = [r[n] + beta * p[n] if n < len(p) else r[n] for n in range(len(r))]
            now = new

    def monomials(c):
        out = [c[-1]]
        for term in c[-2::-1]:
            out = [term - t * out[0]] + [out[n - 1] - t * out[n] for n in range(1, len(out))] + [out[-1]]
        return [jnp.broadcast_to(v[0:1, 0:1], (8, 256)) for v in out]

    cx, cr = monomials(x), monomials(r)
    for k in range(3):
        for s in range(2):
            w = [basis[j, k, s] for j in range(4)]
            mesh_adjoint[k, s] = cx[0] * w[0] + cx[1] * w[1] + cx[2] * w[2]
            residual[k, s] = (cr[0] * w[0] + cr[1] * w[1]) + (cr[2] * w[2] + cr[3] * w[3])


def local(adjoint, flux_jac, shift):
    y, zh = lax.axis_index("y"), lax.axis_index("zh")
    inst = lax.axis_index(("y", "zh"))
    cell = lax.axis_index(("x", "zl", "core"))
    core = lax.axis_index("core")
    pos = jnp.stack([y, zh, inst, cell, core]).astype(jnp.int32)

    lo = send_cell(adjoint[:, :, 1:], 1)
    hi = send_cell(adjoint[:, :, :1], -1)
    eight, ten = (18, 8, 256), (20, 8, 256)
    m0, m1, m2, m3 = call(
        sens_kernel,
        [eight, ten, eight, ten],
        (pos, flux_jac, adjoint, lo, hi, shift),
        [pltpu.VMEM((6, 72, 256), F32)],
    )
    r2, r1, r3 = send_y(m2, 2), send_y(m1, 1), send_y(m3, 3)
    own, out = call(sum_y_kernel, [(12, 8, 256), (13, 8, 256)], (pos, m0, r1, r2, r3, shift))
    (block,) = call(block_kernel, [(4, 2, 16, 256)], (pos, own, send_zh(out), shift))

    even = core == 0
    mate = send_core(block)
    near = send_chip(jnp.where(even, block[:3, 0], block[:3, 1]), -1)
    rows = jnp.where(
        even,
        jnp.concatenate([block[:3, 1:2], mate[:3]], axis=1),
        jnp.concatenate([mate[:3], block[:3, 0:1]], axis=1),
    )
    far = send_chip(jnp.concatenate([rows.reshape(9, 16, 256), mate[3]], axis=0), 1)
    scratch = pltpu.VMEM((3, 8, 16, 256), F32)
    basis, moments = call(
        krylov_kernel,
        [(4, 3, 2, 8, 256), (8, 128)],
        (pos, block, mate, far, near),
        [scratch, scratch],
    )
    parts = lax.all_to_all(jnp.broadcast_to(moments, (16, 8, 128)), ("y", "x"), 0, 0)
    moments = jnp.sum(parts, axis=0)
    parts = lax.all_to_all(jnp.broadcast_to(moments, (16, 8, 128)), ("zh", "zl", "core"), 0, 0)
    shape = (3, 2, 8, 256)
    return tuple(call(finish_kernel, [shape, shape], (pos, parts, basis)))


def solution(mesh):
    fine = Mesh(mesh.devices.reshape(SIZES), AXES)
    inst, cell = ("y", "zh"), ("x", "zl", "core")
    out = P(None, cell, inst, None)
    return jax.shard_map(
        local,
        mesh=fine,
        in_specs=(
            P(inst, None, cell, None, None),
            P(inst, None, None, cell, None, None),
            P(cell, inst, None),
        ),
        out_specs=(out, out),
        check_vma=False,
    )
```

```python
import jax
import jax.numpy as jnp
import numpy as np
from jax import lax
from jax.experimental import pallas as pl
from jax.experimental.pallas import tpu as pltpu
from jax.sharding import Mesh, PartitionSpec as P

ITERS = 3
MU = 1.0
LAME = 1.5
AXES = ("y", "zh", "x", "zl", "core")
SIZES = (4, 2, 4, 4, 2)
F32 = jnp.float32


def flat(at):
    index = 0
    for size, k in zip(SIZES, at):
        index = index * size + k
    return index


def send(v, move):
    pairs = []
    for at in np.ndindex(*SIZES):
        to = move(*at)
        if to is not None:
            pairs.append((flat(at), flat(to)))
    return lax.ppermute(v, AXES, pairs)


def send_y(v, d):
    return send(v, lambda y, zh, x, zl, core: ((y + d) % 4, zh, x, zl, core))


def send_zh(v):
    return send(v, lambda y, zh, x, zl, core: (y, 1 - zh, x, zl, core))


def send_core(v):
    return send(v, lambda y, zh, x, zl, core: (y, zh, x, zl, 1 - core))


def send_pair(v):
    def move(y, zh, x, zl, core):
        q = x * 4 + zl + (1 if core == 1 else -1)
        return (y, zh, q // 4, q % 4, 1 - core) if 0 <= q < 16 else None

    return send(v, move)


VMEM = pl.BlockSpec(memory_space=pltpu.VMEM)
SMEM = pl.BlockSpec(memory_space=pltpu.SMEM)
HBM = pl.BlockSpec(memory_space=pltpu.HBM)


def call(kernel, outs, args, scratch=(), specs=None):
    return pl.pallas_call(
        kernel,
        out_shape=[s if isinstance(s, jax.ShapeDtypeStruct) else jax.ShapeDtypeStruct(s, F32) for s in outs],
        in_specs=[SMEM] + (specs or [VMEM] * (len(args) - 1)),
        out_specs=[VMEM] * len(outs),
        scratch_shapes=list(scratch),
        compiler_params=pltpu.CompilerParams(vmem_limit_bytes=24 * 1024 * 1024),
    )(*args)


def copy_all(pairs, sems):
    copies = [pltpu.make_async_copy(src, dst, sems.at[n]) for n, (src, dst) in enumerate(pairs)]
    for copy in copies:
        copy.start()
    for copy in copies:
        copy.wait()


def split_flux_kernel(pos, f, shift, late, early, near_shift, sems):
    core = pos[4]
    copy_all(
        [(f.at[:, :, :, 1 - core], early), (f.at[:, :, :, core], late), (shift, near_shift)], sems
    )


def sens_of_slab(y, sign, f, a, got, outs, wide):
    zero = jnp.zeros((8, 256), F32)
    for k in range(3):
        wide[k, 0:8, :] = zero
        wide[k, 64:72, :] = zero
    for rows in range(0, 64, 16):
        span = slice(rows, rows + 16)
        total = [None] * 3
        for i in range(2):
            for v in range(5):
                step = got[i, v, span, :].astype(F32) - a[i, v, span, :].astype(F32)
                for k in range(3):
                    term = f[i, v, k, span, :].astype(F32) * step
                    total[k] = term if total[k] is None else total[k] + term
        for k in range(3):
            wide[k, rows + 3 : rows + 19, :] = total[k] * sign
    for d, out in enumerate(outs):
        first = pl.multiple_of(lax.rem(y + d, 4) * 16, 16)
        for k in range(3):
            out[k * 3 : k * 3 + 3] = wide[k, pl.ds(first, 24), :].reshape(3, 8, 256)


def sens_early_kernel(pos, f, a, got, shift, m0, m1, m2, m3, wide):
    sign = jnp.where(pos[4] == 0, 1.0, -1.0)
    sens_of_slab(pos[0], sign, f, a, got, (m0, m1, m2, m3), wide)
    for out in (m1, m3):
        out[9:11] = shift[...]


def sens_late_kernel(pos, f, a, got, m0, m1, m2, m3, wide):
    sign = jnp.where(pos[4] == 0, -1.0, 1.0)
    sens_of_slab(pos[0], sign, f, a, got, (m0, m1, m2, m3), wide)


def sum_y_late_kernel(pos, m0, r1, r2, r3, own, out):
    zh = pos[1]
    for s in range(3):
        for g in range(2):
            for half, to in ((zh, own), (1 - zh, out)):
                k = s * 3 + half + g
                to[s * 2 + g] = (m0[k] + r1[k]) + (r2[k] + r3[k])


def sum_y_early_kernel(pos, m0, r1, r2, r3, shift, after, own, out):
    sum_y_late_kernel(pos, m0, r1, r2, r3, own, out)
    low = pos[1] == 0
    for x in range(2):
        below = jnp.where(low, shift[x, 6:8, :], r1[9 + x, 6:8, :])
        above = jnp.where(low, r3[9 + x, 0:2, :], shift[x, 0:2, :])
        out[6, x * 4 : x * 4 + 2, :] = below
        out[6, x * 4 + 2 : x * 4 + 4, :] = above


def block_late_kernel(pos, own, got, block):
    for s in range(3):
        for g in range(2):
            block[s, g * 8 : g * 8 + 8, :] = own[s * 2 + g] + got[s * 2 + g]


def block_early_kernel(pos, own, got, shift, after, block):
    block_late_kernel(pos, own, got, block)
    for x in range(2):
        block[3 + x, 0:8, :] = jnp.zeros((8, 256), F32)
        block[3 + x, 8:16, :] = jnp.zeros((8, 256), F32)
        block[3 + x, 3:11, :] = shift[x]
        block[3 + x, 1:3, :] = got[6, x * 4 : x * 4 + 2, :]
        block[3 + x, 11:13, :] = got[6, x * 4 + 2 : x * 4 + 4, :]


def krylov_kernel(pos, early, late, mate_early, far_early, far_late, mate_late, basis, moments, w0, w1, w2, sh):
    inst, cell, core = pos[2], pos[3], pos[4]

    def place(x):
        return x + core * (7 - 2 * x)

    for k in range(3):
        line = (
            far_early[3 + k], far_early[k], far_late[k], late[k],
            early[k], mate_early[k], mate_late[k], mate_late[3 + k],
        )
        for x in range(8):
            w0[k, place(x)] = line[x]
    for x in range(2):
        sh[1 + core * 4 + x] = far_early[6 + x]
        sh[3 + x] = early[3 + x]
        sh[5 - core * 4 + x] = mate_early[3 + x]

    row = lax.broadcasted_iota(jnp.int32, (16, 256), 0) + (inst * 8 - 3)
    lane = lax.broadcasted_iota(jnp.int32, (16, 256), 1)
    in_row = (row >= 0) & (row < 64)
    first, last = lane == 0, lane == 255

    def inside(x):
        at = cell * 2 - 3 + x
        return in_row & jnp.broadcast_to((at >= 0) & (at < 64), (16, 256))

    def y_up(v):
        return pltpu.roll(v, 15, 0)

    def y_down(v):
        return pltpu.roll(v, 1, 0)

    def z_up(v):
        return jnp.where(last, 0.0, pltpu.roll(v, 255, 1))

    def z_down(v):
        return jnp.where(first, 0.0, pltpu.roll(v, 1, 1))

    def apply(u, lo, hi, keep):
        before = None
        for x in range(lo - 1, hi + 1):
            c = [u(k, x) for k in range(3)]
            u1y, u2z = y_up(c[1]), z_up(c[2])
            dv = (u(0, x + 1) - c[0]) + (u1y - c[1]) + (u2z - c[2])
            mask = inside(x)
            dv = jnp.where(mask, dv, 0.0)
            if x >= lo:
                ups = [(y_up(c[0]), z_up(c[0])), (u1y, z_up(c[1])), (y_up(c[2]), u2z)]
                grads = [before, y_down(dv), z_down(dv)]
                weight = sh[x] + 6.0 * MU
                for k in range(3):
                    beside = (u(k, x + 1) + u(k, x - 1)) + (ups[k][0] + y_down(c[k]))
                    beside = beside + (ups[k][1] + z_down(c[k]))
                    image = weight * c[k] - MU * beside + LAME * (grads[k] - dv)
                    keep(k, x, jnp.where(mask, image, 0.0))
            before = dv

    def put(ref):
        def keep(k, x, v):
            ref[k, x] = v

        return keep

    apply(lambda k, x: w0[k, x], 1, 6, put(w1))
    apply(lambda k, x: w1[k, x], 2, 5, put(w2))
    sums = [None] * 6

    def finish(k, x, v):
        w = [w0[k, x, 3:11, :], w1[k, x, 3:11, :], w2[k, x, 3:11, :], v[3:11, :]]
        for j in range(4):
            basis[j, k, x - 3] = w[j]
        for n, (i, j) in enumerate(((0, 0), (0, 1), (1, 1), (1, 2), (2, 2), (2, 3))):
            term = w[i] * w[j]
            sums[n] = term if sums[n] is None else sums[n] + term

    apply(lambda k, x: w2[k, x], 3, 4, finish)
    moments[...] = jnp.zeros((8, 128), F32)
    for n in range(6):
        line = jnp.sum(sums[n], axis=0, keepdims=True)
        moments[n : n + 1, :] = line[:, :128] + line[:, 128:]


def two_sum(a, b):
    s = a + b
    t = s - a
    return s, (a - (s - t)) + (b - t)


def two_product(a, b):
    def halves(v):
        t = 4097.0 * v
        high = t - (t - v)
        return high, v - high

    p = a * b
    ah, al = halves(a)
    bh, bl = halves(b)
    return p, ((ah * bh - p) + ah * bl + al * bh) + al * bl


def finish_kernel(pos, parts, basis, mesh_adjoint, residual):
    high = parts[0]
    low = jnp.zeros((8, 128), F32)
    for n in range(1, parts.shape[0]):
        high, error = two_sum(high, parts[n])
        low = low + error
    for step in (64, 32, 16, 8, 4, 2, 1):
        high, error = two_sum(high, pltpu.roll(high, step, 1))
        low = (low + pltpu.roll(low, step, 1)) + error

    def line(v, n):
        return jnp.broadcast_to(v[n : n + 1, :], (8, 128))

    t = line(high, 1) / line(high, 0)
    centred = [line(high, 0) + line(low, 0)]
    for n in range(1, 6):
        product, error = two_product(t, high)
        error = error + t * low
        high, more = two_sum(pltpu.roll(high, 7, 0), -product)
        low = (pltpu.roll(low, 7, 0) - error) + more
        high, low = two_sum(high, low)
        centred.append(line(high, 0) + line(low, 0))

    def dot(u, v):
        total = None
        for i, p in enumerate(u):
            for j, q in enumerate(v):
                term = p * q * centred[i + j]
                total = term if total is None else total + term
        return total

    one = jnp.ones((8, 128), F32)
    r, p, x, now = [one], [one], [], centred[0]
    for sweep in range(ITERS):
        image = [t * p[0]] + [p[n - 1] + t * p[n] for n in range(1, len(p))] + [p[-1]]
        alpha = now / dot(p, image)
        x = [x[n] + alpha * p[n] if n < len(x) else alpha * p[n] for n in range(len(p))]
        r = [r[n] - alpha * image[n] if n < len(r) else -alpha * image[n] for n in range(len(image))]
        if sweep < ITERS - 1:
            new = dot(r, r)
            beta = new / now
            p = [r[n] + beta * p[n] if n < len(p) else r[n] for n in range(len(r))]
            now = new

    def monomials(c):
        out = [c[-1]]
        for term in c[-2::-1]:
            out = [term - t * out[0]] + [out[n - 1] - t * out[n] for n in range(1, len(out))] + [out[-1]]
        return [jnp.broadcast_to(v[0:1, 0:1], (8, 256)) for v in out]

    cx, cr = monomials(x), monomials(r)
    for k in range(3):
        for s in range(2):
            w = [basis[j, k, s] for j in range(4)]
            mesh_adjoint[k, s] = cx[0] * w[0] + cx[1] * w[1] + cx[2] * w[2]
            residual[k, s] = (cr[0] * w[0] + cr[1] * w[1]) + (cr[2] * w[2] + cr[3] * w[3])


def local(adjoint, flux_jac, shift):
    y, zh = lax.axis_index("y"), lax.axis_index("zh")
    inst = lax.axis_index(("y", "zh"))
    cell = lax.axis_index(("x", "zl", "core"))
    core = lax.axis_index("core")
    pos = jnp.stack([y, zh, inst, cell, core]).astype(jnp.int32)

    slab_flux = jax.ShapeDtypeStruct((2, 5, 3, 64, 256), jnp.bfloat16)
    outer = lax.dynamic_index_in_dim(adjoint, core, 2, False)
    inner = lax.dynamic_index_in_dim(adjoint, 1 - core, 2, False)
    got_outer = send_pair(outer)
    got_inner = send_core(inner)
    flux_late, flux_early, shift = call(
        split_flux_kernel,
        [slab_flux, slab_flux, (2, 8, 256)],
        (pos, flux_jac, shift),
        [pltpu.SemaphoreType.DMA((3,))],
        [HBM, HBM],
    )

    nine, eleven = (9, 8, 256), (11, 8, 256)
    wide = [pltpu.VMEM((3, 72, 256), F32)]
    m0, m1, m2, m3 = call(
        sens_early_kernel,
        [nine, eleven, nine, eleven],
        (pos, flux_early, outer, got_inner, shift),
        wide,
    )
    r2, r1, r3 = send_y(m2, 2), send_y(m1, 1), send_y(m3, 3)
    n0, n1, n2, n3 = call(sens_late_kernel, [nine] * 4, (pos, flux_late, inner, got_outer), wide)
    q2, q1, q3 = send_y(n2, 2), send_y(n1, 1), send_y(n3, 3)
    six, seven = (6, 8, 256), (7, 8, 256)
    own, out = call(sum_y_early_kernel, [six, seven], (pos, m0, r1, r2, r3, shift, n0))
    got = send_zh(out)
    own_late, out_late = call(sum_y_late_kernel, [six, six], (pos, n0, q1, q2, q3))
    got_late = send_zh(out_late)
    (early,) = call(block_early_kernel, [(5, 16, 256)], (pos, own, got, shift, own_late))
    mate_early = send_core(early)
    far_early = send_pair(jnp.concatenate([early[:3], mate_early[:3], early[3:]], axis=0))
    (late,) = call(block_late_kernel, [(3, 16, 256)], (pos, own_late, got_late))
    far_late = send_pair(late)
    mate_late = send_core(jnp.concatenate([late, far_late], axis=0))

    scratch = pltpu.VMEM((3, 8, 16, 256), F32)
    basis, moments = call(
        krylov_kernel,
        [(4, 3, 2, 8, 256), (8, 128)],
        (pos, early, late, mate_early, far_early, far_late, mate_late),
        [scratch, scratch, scratch, pltpu.VMEM((8, 16, 256), F32)],
    )
    parts = lax.all_to_all(jnp.broadcast_to(moments, (16, 8, 128)), ("y", "x"), 0, 0)
    moments = jnp.sum(parts, axis=0)
    parts = lax.all_to_all(jnp.broadcast_to(moments, (16, 8, 128)), ("zh", "zl", "core"), 0, 0)
    shape = (3, 2, 8, 256)
    return tuple(call(finish_kernel, [shape, shape], (pos, parts, basis)))


def solution(mesh):
    fine = Mesh(mesh.devices.reshape(SIZES), AXES)
    inst, cell = ("y", "zh"), ("x", "zl", "core")
    out = P(None, cell, inst, None)
    return jax.shard_map(
        local,
        mesh=fine,
        in_specs=(
            P(inst, None, cell, None, None),
            P(inst, None, None, cell, None, None),
            P(cell, inst, None),
        ),
        out_specs=(out, out),
        check_vma=False,
    )
```

```python
import jax
import jax.numpy as jnp
import numpy as np
from jax import lax
from jax.experimental import pallas as pl
from jax.experimental.pallas import tpu as pltpu
from jax.sharding import Mesh, PartitionSpec as P

ITERS = 3
MU = 1.0
LAME = 1.5
AXES = ("y", "zh", "x", "zl", "core")
SIZES = (4, 2, 4, 4, 2)
F32 = jnp.float32


def flat(at):
    index = 0
    for size, k in zip(SIZES, at):
        index = index * size + k
    return index


def send(v, move):
    pairs = []
    for at in np.ndindex(*SIZES):
        to = move(*at)
        if to is not None:
            pairs.append((flat(at), flat(to)))
    return lax.ppermute(v, AXES, pairs)


def send_y(v, d):
    return send(v, lambda y, zh, x, zl, core: ((y + d) % 4, zh, x, zl, core))


def send_zh(v):
    return send(v, lambda y, zh, x, zl, core: (y, 1 - zh, x, zl, core))


def send_core(v):
    return send(v, lambda y, zh, x, zl, core: (y, zh, x, zl, 1 - core))


def send_pair(v):
    def move(y, zh, x, zl, core):
        q = x * 4 + zl + (1 if core == 1 else -1)
        return (y, zh, q // 4, q % 4, 1 - core) if 0 <= q < 16 else None

    return send(v, move)


VMEM = pl.BlockSpec(memory_space=pltpu.VMEM)
SMEM = pl.BlockSpec(memory_space=pltpu.SMEM)


def call(kernel, outs, args, scratch=()):
    return pl.pallas_call(
        kernel,
        out_shape=[jax.ShapeDtypeStruct(s, F32) for s in outs],
        in_specs=[SMEM] + [VMEM] * (len(args) - 1),
        out_specs=[VMEM] * len(outs),
        scratch_shapes=list(scratch),
        compiler_params=pltpu.CompilerParams(vmem_limit_bytes=24 * 1024 * 1024),
    )(*args)


def sens_of_slab(y, slab, sign, f, a, got, outs, wide):
    zero = jnp.zeros((8, 256), F32)
    for k in range(3):
        wide[k, 0:8, :] = zero
        wide[k, 64:72, :] = zero
    for rows in range(0, 64, 16):
        span = slice(rows, rows + 16)
        total = [None] * 3
        for i in range(2):
            for v in range(5):
                step = got[i, v, span, :].astype(F32) - a[i, v, span, :].astype(F32)
                for k in range(3):
                    term = f[i, v, k, slab, span, :].astype(F32) * step
                    total[k] = term if total[k] is None else total[k] + term
        for k in range(3):
            wide[k, rows + 3 : rows + 19, :] = total[k] * sign
    for d, out in enumerate(outs):
        first = pl.multiple_of(lax.rem(y + d, 4) * 16, 16)
        for k in range(3):
            out[k * 3 : k * 3 + 3] = wide[k, pl.ds(first, 24), :].reshape(3, 8, 256)


def sens_early_kernel(pos, f, a, got, shift, m0, m1, m2, m3, wide):
    sign = jnp.where(pos[4] == 0, 1.0, -1.0)
    sens_of_slab(pos[0], 1 - pos[4], sign, f, a, got, (m0, m1, m2, m3), wide)
    for out in (m1, m3):
        out[9:11] = shift[...]


def sens_late_kernel(pos, f, a, got, after, m0, m1, m2, m3, wide):
    sign = jnp.where(pos[4] == 0, -1.0, 1.0)
    sens_of_slab(pos[0], pos[4], sign, f, a, got, (m0, m1, m2, m3), wide)


def sum_y_kernel(pos, m0, r1, r2, r3, n0, q1, q2, q3, shift, own, out):
    zh = pos[1]
    for first, (p0, p1, p2, p3) in ((0, (m0, r1, r2, r3)), (6, (n0, q1, q2, q3))):
        for s in range(3):
            for g in range(2):
                for half, to in ((zh, own), (1 - zh, out)):
                    k = s * 3 + half + g
                    to[first + s * 2 + g] = (p0[k] + p1[k]) + (p2[k] + p3[k])
    low = zh == 0
    for x in range(2):
        below = jnp.where(low, shift[x, 6:8, :], r1[9 + x, 6:8, :])
        above = jnp.where(low, r3[9 + x, 0:2, :], shift[x, 0:2, :])
        out[12, x * 4 : x * 4 + 2, :] = below
        out[12, x * 4 + 2 : x * 4 + 4, :] = above


def block_kernel(pos, own, got, shift, block):
    for s in range(6):
        for g in range(2):
            block[s, g * 8 : g * 8 + 8, :] = own[s * 2 + g] + got[s * 2 + g]
    for x in range(2):
        block[6 + x, 0:8, :] = jnp.zeros((8, 256), F32)
        block[6 + x, 8:16, :] = jnp.zeros((8, 256), F32)
        block[6 + x, 3:11, :] = shift[x]
        block[6 + x, 1:3, :] = got[12, x * 4 : x * 4 + 2, :]
        block[6 + x, 11:13, :] = got[12, x * 4 + 2 : x * 4 + 4, :]


def krylov_kernel(pos, block, mate, far, beyond, basis, moments, w0, w1, w2, sh):
    inst, cell, core = pos[2], pos[3], pos[4]

    def place(x):
        return x + core * (7 - 2 * x)

    for k in range(3):
        line = (
            far[8 + k], far[k], far[3 + k], block[3 + k],
            block[k], mate[k], mate[3 + k], beyond[k],
        )
        for x in range(8):
            w0[k, place(x)] = line[x]
    for x in range(2):
        sh[1 + core * 4 + x] = far[6 + x]
        sh[3 + x] = block[6 + x]
        sh[5 - core * 4 + x] = mate[6 + x]

    row = lax.broadcasted_iota(jnp.int32, (16, 256), 0) + (inst * 8 - 3)
    lane = lax.broadcasted_iota(jnp.int32, (16, 256), 1)
    in_row = (row >= 0) & (row < 64)
    first, last = lane == 0, lane == 255

    def inside(x):
        at = cell * 2 - 3 + x
        return in_row & jnp.broadcast_to((at >= 0) & (at < 64), (16, 256))

    def y_up(v):
        return pltpu.roll(v, 15, 0)

    def y_down(v):
        return pltpu.roll(v, 1, 0)

    def z_up(v):
        return jnp.where(last, 0.0, pltpu.roll(v, 255, 1))

    def z_down(v):
        return jnp.where(first, 0.0, pltpu.roll(v, 1, 1))

    def apply(u, lo, hi, keep):
        before = None
        for x in range(lo - 1, hi + 1):
            c = [u(k, x) for k in range(3)]
            u1y, u2z = y_up(c[1]), z_up(c[2])
            dv = (u(0, x + 1) - c[0]) + (u1y - c[1]) + (u2z - c[2])
            mask = inside(x)
            dv = jnp.where(mask, dv, 0.0)
            if x >= lo:
                ups = [(y_up(c[0]), z_up(c[0])), (u1y, z_up(c[1])), (y_up(c[2]), u2z)]
                grads = [before, y_down(dv), z_down(dv)]
                weight = sh[x] + 6.0 * MU
                for k in range(3):
                    beside = (u(k, x + 1) + u(k, x - 1)) + (ups[k][0] + y_down(c[k]))
                    beside = beside + (ups[k][1] + z_down(c[k]))
                    image = weight * c[k] - MU * beside + LAME * (grads[k] - dv)
                    keep(k, x, jnp.where(mask, image, 0.0))
            before = dv

    def put(ref):
        def keep(k, x, v):
            ref[k, x] = v

        return keep

    apply(lambda k, x: w0[k, x], 1, 6, put(w1))
    apply(lambda k, x: w1[k, x], 2, 5, put(w2))
    sums = [None] * 6

    def finish(k, x, v):
        w = [w0[k, x, 3:11, :], w1[k, x, 3:11, :], w2[k, x, 3:11, :], v[3:11, :]]
        for j in range(4):
            basis[j, k, x - 3] = w[j]
        for n, (i, j) in enumerate(((0, 0), (0, 1), (1, 1), (1, 2), (2, 2), (2, 3))):
            term = w[i] * w[j]
            sums[n] = term if sums[n] is None else sums[n] + term

    apply(lambda k, x: w2[k, x], 3, 4, finish)
    moments[...] = jnp.zeros((8, 128), F32)
    for n in range(6):
        line = jnp.sum(sums[n], axis=0, keepdims=True)
        moments[n : n + 1, :] = line[:, :128] + line[:, 128:]


def two_sum(a, b):
    s = a + b
    t = s - a
    return s, (a - (s - t)) + (b - t)


def two_product(a, b):
    def halves(v):
        t = 4097.0 * v
        high = t - (t - v)
        return high, v - high

    p = a * b
    ah, al = halves(a)
    bh, bl = halves(b)
    return p, ((ah * bh - p) + ah * bl + al * bh) + al * bl


def finish_kernel(pos, parts, basis, mesh_adjoint, residual):
    sums = [(parts[n], None) for n in range(parts.shape[0])]
    while len(sums) > 1:
        pairs = []
        for (p, rest), (q, more_rest) in zip(sums[::2], sums[1::2]):
            high, low = two_sum(p, q)
            pairs.append((high, low if rest is None else low + (rest + more_rest)))
        sums = pairs
    high, low = sums[0]
    for step in (64, 32, 16, 8, 4, 2, 1):
        high, error = two_sum(high, pltpu.roll(high, step, 1))
        low = (low + pltpu.roll(low, step, 1)) + error

    def line(v, n):
        return jnp.broadcast_to(v[n : n + 1, :], (8, 128))

    t = line(high, 1) / line(high, 0)
    centred = [line(high, 0) + line(low, 0)]
    for n in range(1, 6):
        product, error = two_product(t, high)
        error = error + t * low
        high, more = two_sum(pltpu.roll(high, 7, 0), -product)
        low = (pltpu.roll(low, 7, 0) - error) + more
        high, low = two_sum(high, low)
        centred.append(line(high, 0) + line(low, 0))

    def dot(u, v):
        total = None
        for i, p in enumerate(u):
            for j, q in enumerate(v):
                term = p * q * centred[i + j]
                total = term if total is None else total + term
        return total

    one = jnp.ones((8, 128), F32)
    r, p, x, now = [one], [one], [], centred[0]
    for sweep in range(ITERS):
        image = [t * p[0]] + [p[n - 1] + t * p[n] for n in range(1, len(p))] + [p[-1]]
        alpha = now / dot(p, image)
        x = [x[n] + alpha * p[n] if n < len(x) else alpha * p[n] for n in range(len(p))]
        r = [r[n] - alpha * image[n] if n < len(r) else -alpha * image[n] for n in range(len(image))]
        if sweep < ITERS - 1:
            new = dot(r, r)
            beta = new / now
            p = [r[n] + beta * p[n] if n < len(p) else r[n] for n in range(len(r))]
            now = new

    def monomials(c):
        out = [c[-1]]
        for term in c[-2::-1]:
            out = [term - t * out[0]] + [out[n - 1] - t * out[n] for n in range(1, len(out))] + [out[-1]]
        return [jnp.broadcast_to(v[0:1, 0:1], (8, 256)) for v in out]

    cx, cr = monomials(x), monomials(r)
    for k in range(3):
        for s in range(2):
            w = [basis[j, k, s] for j in range(4)]
            mesh_adjoint[k, s] = cx[0] * w[0] + cx[1] * w[1] + cx[2] * w[2]
            residual[k, s] = (cr[0] * w[0] + cr[1] * w[1]) + (cr[2] * w[2] + cr[3] * w[3])


def local(adjoint, flux_jac, shift):
    y, zh = lax.axis_index("y"), lax.axis_index("zh")
    inst = lax.axis_index(("y", "zh"))
    cell = lax.axis_index(("x", "zl", "core"))
    core = lax.axis_index("core")
    pos = jnp.stack([y, zh, inst, cell, core]).astype(jnp.int32)

    outer = lax.dynamic_index_in_dim(adjoint, core, 2, False)
    inner = lax.dynamic_index_in_dim(adjoint, 1 - core, 2, False)
    got_outer = send_pair(outer)
    got_inner = send_core(inner)

    nine, eleven = (9, 8, 256), (11, 8, 256)
    wide = [pltpu.VMEM((3, 72, 256), F32)]
    m0, m1, m2, m3 = call(
        sens_early_kernel,
        [nine, eleven, nine, eleven],
        (pos, flux_jac, outer, got_inner, shift),
        wide,
    )
    r2, r1, r3 = send_y(m2, 2), send_y(m1, 1), send_y(m3, 3)
    n0, n1, n2, n3 = call(sens_late_kernel, [nine] * 4, (pos, flux_jac, inner, got_outer, m0), wide)
    q2, q1, q3 = send_y(n2, 2), send_y(n1, 1), send_y(n3, 3)
    own, out = call(
        sum_y_kernel, [(12, 8, 256), (13, 8, 256)], (pos, m0, r1, r2, r3, n0, q1, q2, q3, shift)
    )
    (block,) = call(block_kernel, [(8, 16, 256)], (pos, own, send_zh(out), shift))
    mate = send_core(block)
    far = send_pair(jnp.concatenate([block, mate[:3]], axis=0))
    beyond = send_core(far[3:6])

    scratch = pltpu.VMEM((3, 8, 16, 256), F32)
    basis, moments = call(
        krylov_kernel,
        [(4, 3, 2, 8, 256), (8, 128)],
        (pos, block, mate, far, beyond),
        [scratch, scratch, scratch, pltpu.VMEM((8, 16, 256), F32)],
    )
    parts = lax.all_to_all(jnp.broadcast_to(moments, (16, 8, 128)), ("y", "x"), 0, 0)
    moments = jnp.sum(parts, axis=0)
    parts = lax.all_to_all(jnp.broadcast_to(moments, (16, 8, 128)), ("zh", "zl", "core"), 0, 0)
    shape = (3, 2, 8, 256)
    return tuple(call(finish_kernel, [shape, shape], (pos, parts, basis)))


def solution(mesh):
    fine = Mesh(mesh.devices.reshape(SIZES), AXES)
    inst, cell = ("y", "zh"), ("x", "zl", "core")
    out = P(None, cell, inst, None)
    return jax.shard_map(
        local,
        mesh=fine,
        in_specs=(
            P(inst, None, cell, None, None),
            P(inst, None, None, cell, None, None),
            P(cell, inst, None),
        ),
        out_specs=(out, out),
        check_vma=False,
    )
```

```python
import jax
import jax.numpy as jnp
import numpy as np
from jax import lax
from jax.experimental import pallas as pl
from jax.experimental.pallas import tpu as pltpu
from jax.sharding import Mesh, PartitionSpec as P

ITERS = 3
MU = 1.0
LAME = 1.5
AXES = ("y", "zh", "x", "zl", "core")
SIZES = (4, 2, 4, 4, 2)
F32 = jnp.float32


def flat(at):
    index = 0
    for size, k in zip(SIZES, at):
        index = index * size + k
    return index


def send(v, move):
    pairs = []
    for at in np.ndindex(*SIZES):
        to = move(*at)
        if to is not None:
            pairs.append((flat(at), flat(to)))
    return lax.ppermute(v, AXES, pairs)


def send_y(v, d):
    return send(v, lambda y, zh, x, zl, core: ((y + d) % 4, zh, x, zl, core))


def send_zh(v):
    return send(v, lambda y, zh, x, zl, core: (y, 1 - zh, x, zl, core))


def send_core(v):
    return send(v, lambda y, zh, x, zl, core: (y, zh, x, zl, 1 - core))


def send_pair(v):
    def move(y, zh, x, zl, core):
        q = x * 4 + zl + (1 if core == 1 else -1)
        return (y, zh, q // 4, q % 4, 1 - core) if 0 <= q < 16 else None

    return send(v, move)


VMEM = pl.BlockSpec(memory_space=pltpu.VMEM)


def call(kernel, outs, args, scratch=()):
    return pl.pallas_call(
        kernel,
        out_shape=[jax.ShapeDtypeStruct(s, F32) for s in outs],
        in_specs=[VMEM] * len(args),
        out_specs=[VMEM] * len(outs),
        scratch_shapes=list(scratch),
        compiler_params=pltpu.CompilerParams(vmem_limit_bytes=24 * 1024 * 1024),
    )(*args)


def sens_of_slab(slab, sign, f, a, got, wide):
    zero = jnp.zeros((8, 256), F32)
    for k in range(3):
        wide[k, 0:8, :] = zero
        wide[k, 64:72, :] = zero
    for rows in range(0, 64, 16):
        span = slice(rows, rows + 16)
        total = [None] * 3
        for i in range(2):
            for v in range(5):
                step = got[i, v, span, :].astype(F32) - a[i, v, span, :].astype(F32)
                for k in range(3):
                    term = f[i, v, k, slab, span, :].astype(F32) * step
                    total[k] = term if total[k] is None else total[k] + term
        for k in range(3):
            wide[k, rows + 3 : rows + 19, :] = total[k] * sign


def sens_early_kernel(f, a, got, wide):
    core = lax.axis_index("core")
    sens_of_slab(1 - core, jnp.where(core == 0, 1.0, -1.0), f, a, got, wide)


def sens_late_kernel(f, a, got, early, shift, m0, m1, m2, m3, wide):
    y, core = lax.axis_index("y"), lax.axis_index("core")
    sens_of_slab(core, jnp.where(core == 0, -1.0, 1.0), f, a, got, wide)
    for d, out in enumerate((m0, m1, m2, m3)):
        first = pl.multiple_of(lax.rem(y + d, 4) * 16, 16)
        for k in range(3):
            out[k * 3 : k * 3 + 3] = early[k, pl.ds(first, 24), :].reshape(3, 8, 256)
            out[9 + k * 3 : 12 + k * 3] = wide[k, pl.ds(first, 24), :].reshape(3, 8, 256)
    for out in (m1, m3):
        out[18:20] = shift[...]


def sum_y_kernel(m0, r1, r2, r3, shift, own, out):
    zh = lax.axis_index("zh")
    for s in range(6):
        for g in range(2):
            for half, to in ((zh, own), (1 - zh, out)):
                k = s * 3 + half + g
                to[s * 2 + g] = (m0[k] + r1[k]) + (r2[k] + r3[k])
    low = zh == 0
    for x in range(2):
        below = jnp.where(low, shift[x, 6:8, :], r1[18 + x, 6:8, :])
        above = jnp.where(low, r3[18 + x, 0:2, :], shift[x, 0:2, :])
        out[12, x * 4 : x * 4 + 2, :] = below
        out[12, x * 4 + 2 : x * 4 + 4, :] = above


def krylov_kernel(block, mate, far, beyond, basis, moments, w0, w1, w2, sh):
    core = lax.axis_index("core")
    inst = lax.axis_index("y") * 2 + lax.axis_index("zh")
    cell = lax.axis_index("x") * 8 + lax.axis_index("zl") * 2 + core

    def place(x):
        return x + core * (7 - 2 * x)

    for k in range(3):
        line = (
            far[8 + k], far[k], far[3 + k], block[3 + k],
            block[k], mate[k], mate[3 + k], beyond[k],
        )
        for x in range(8):
            w0[k, place(x)] = line[x]
    for x in range(2):
        sh[1 + core * 4 + x] = far[6 + x]
        sh[3 + x] = block[6 + x]
        sh[5 - core * 4 + x] = mate[6 + x]

    row = lax.broadcasted_iota(jnp.int32, (16, 256), 0) + (inst * 8 - 3)
    lane = lax.broadcasted_iota(jnp.int32, (16, 256), 1)
    in_row = (row >= 0) & (row < 64)
    first, last = lane == 0, lane == 255

    def inside(x):
        at = cell * 2 - 3 + x
        return in_row & jnp.broadcast_to((at >= 0) & (at < 64), (16, 256))

    def y_up(v):
        return pltpu.roll(v, 15, 0)

    def y_down(v):
        return pltpu.roll(v, 1, 0)

    def z_up(v):
        return jnp.where(last, 0.0, pltpu.roll(v, 255, 1))

    def z_down(v):
        return jnp.where(first, 0.0, pltpu.roll(v, 1, 1))

    def apply(u, lo, hi, keep):
        before = None
        for x in range(lo - 1, hi + 1):
            c = [u(k, x) for k in range(3)]
            u1y, u2z = y_up(c[1]), z_up(c[2])
            dv = (u(0, x + 1) - c[0]) + (u1y - c[1]) + (u2z - c[2])
            mask = inside(x)
            dv = jnp.where(mask, dv, 0.0)
            if x >= lo:
                ups = [(y_up(c[0]), z_up(c[0])), (u1y, z_up(c[1])), (y_up(c[2]), u2z)]
                grads = [before, y_down(dv), z_down(dv)]
                weight = sh[x] + 6.0 * MU
                for k in range(3):
                    beside = (u(k, x + 1) + u(k, x - 1)) + (ups[k][0] + y_down(c[k]))
                    beside = beside + (ups[k][1] + z_down(c[k]))
                    image = weight * c[k] - MU * beside + LAME * (grads[k] - dv)
                    keep(k, x, jnp.where(mask, image, 0.0))
            before = dv

    def put(ref):
        def keep(k, x, v):
            ref[k, x] = v

        return keep

    apply(lambda k, x: w0[k, x], 1, 6, put(w1))
    apply(lambda k, x: w1[k, x], 2, 5, put(w2))
    sums = [None] * 6

    def finish(k, x, v):
        w = [w0[k, x, 3:11, :], w1[k, x, 3:11, :], w2[k, x, 3:11, :], v[3:11, :]]
        for j in range(4):
            basis[j, k, x - 3] = w[j]
        for n, (i, j) in enumerate(((0, 0), (0, 1), (1, 1), (1, 2), (2, 2), (2, 3))):
            term = w[i] * w[j]
            sums[n] = term if sums[n] is None else sums[n] + term

    apply(lambda k, x: w2[k, x], 3, 4, finish)
    moments[...] = jnp.zeros((8, 128), F32)
    for n in range(6):
        line = jnp.sum(sums[n], axis=0, keepdims=True)
        moments[n : n + 1, :] = line[:, :128] + line[:, 128:]


def two_sum(a, b):
    s = a + b
    t = s - a
    return s, (a - (s - t)) + (b - t)


def two_product(a, b):
    def halves(v):
        t = 4097.0 * v
        high = t - (t - v)
        return high, v - high

    p = a * b
    ah, al = halves(a)
    bh, bl = halves(b)
    return p, ((ah * bh - p) + ah * bl + al * bh) + al * bl


def finish_kernel(parts, basis, mesh_adjoint, residual):
    sums = [(parts[n], None) for n in range(parts.shape[0])]
    while len(sums) > 1:
        pairs = []
        for (p, rest), (q, more_rest) in zip(sums[::2], sums[1::2]):
            high, low = two_sum(p, q)
            pairs.append((high, low if rest is None else low + (rest + more_rest)))
        sums = pairs
    high, low = sums[0]
    for step in (64, 32, 16, 8, 4, 2, 1):
        high, error = two_sum(high, pltpu.roll(high, step, 1))
        low = (low + pltpu.roll(low, step, 1)) + error

    def line(v, n):
        return jnp.broadcast_to(v[n : n + 1, :], (8, 128))

    t = line(high, 1) / line(high, 0)
    centred = [line(high, 0) + line(low, 0)]
    for n in range(1, 6):
        product, error = two_product(t, high)
        error = error + t * low
        high, more = two_sum(pltpu.roll(high, 7, 0), -product)
        low = (pltpu.roll(low, 7, 0) - error) + more
        high, low = two_sum(high, low)
        centred.append(line(high, 0) + line(low, 0))

    def dot(u, v):
        total = None
        for i, p in enumerate(u):
            for j, q in enumerate(v):
                term = p * q * centred[i + j]
                total = term if total is None else total + term
        return total

    one = jnp.ones((8, 128), F32)
    r, p, x, now = [one], [one], [], centred[0]
    for sweep in range(ITERS):
        image = [t * p[0]] + [p[n - 1] + t * p[n] for n in range(1, len(p))] + [p[-1]]
        alpha = now / dot(p, image)
        x = [x[n] + alpha * p[n] if n < len(x) else alpha * p[n] for n in range(len(p))]
        r = [r[n] - alpha * image[n] if n < len(r) else -alpha * image[n] for n in range(len(image))]
        if sweep < ITERS - 1:
            new = dot(r, r)
            beta = new / now
            p = [r[n] + beta * p[n] if n < len(p) else r[n] for n in range(len(r))]
            now = new

    def monomials(c):
        out = [c[-1]]
        for term in c[-2::-1]:
            out = [term - t * out[0]] + [out[n - 1] - t * out[n] for n in range(1, len(out))] + [out[-1]]
        return [jnp.broadcast_to(v[0:1, 0:1], (8, 256)) for v in out]

    cx, cr = monomials(x), monomials(r)
    for k in range(3):
        for s in range(2):
            w = [basis[j, k, s] for j in range(4)]
            mesh_adjoint[k, s] = cx[0] * w[0] + cx[1] * w[1] + cx[2] * w[2]
            residual[k, s] = (cr[0] * w[0] + cr[1] * w[1]) + (cr[2] * w[2] + cr[3] * w[3])


def local(adjoint, flux_jac, shift):
    core = lax.axis_index("core")
    outer = lax.dynamic_index_in_dim(adjoint, core, 2, False)
    inner = lax.dynamic_index_in_dim(adjoint, 1 - core, 2, False)
    got_outer = send_pair(outer)
    got_inner = send_core(inner)

    rows = (3, 72, 256)
    (early,) = call(sens_early_kernel, [rows], (flux_jac, outer, got_inner))
    eight, ten = (18, 8, 256), (20, 8, 256)
    m0, m1, m2, m3 = call(
        sens_late_kernel,
        [eight, ten, eight, ten],
        (flux_jac, inner, got_outer, early, shift),
        [pltpu.VMEM(rows, F32)],
    )
    r2, r1, r3 = send_y(m2, 2), send_y(m1, 1), send_y(m3, 3)
    own, out = call(sum_y_kernel, [(12, 8, 256), (13, 8, 256)], (m0, r1, r2, r3, shift))
    got = send_zh(out)
    sides = got[12].reshape(2, 4, 256)
    ends = [jnp.zeros((2, n, 256), F32) for n in (1, 3)]
    wider = jnp.concatenate([ends[0], sides[:, :2], shift, sides[:, 2:], ends[1]], axis=1)
    block = jnp.concatenate([(own + got[:12]).reshape(6, 16, 256), wider], axis=0)
    mate = send_core(block)
    far = send_pair(jnp.concatenate([block, mate[:3]], axis=0))
    beyond = send_core(far[3:6])

    scratch = pltpu.VMEM((3, 8, 16, 256), F32)
    basis, moments = call(
        krylov_kernel,
        [(4, 3, 2, 8, 256), (8, 128)],
        (block, mate, far, beyond),
        [scratch, scratch, scratch, pltpu.VMEM((8, 16, 256), F32)],
    )
    parts = lax.all_to_all(jnp.broadcast_to(moments, (16, 8, 128)), ("y", "x"), 0, 0)
    moments = jnp.sum(parts, axis=0)
    parts = lax.all_to_all(jnp.broadcast_to(moments, (16, 8, 128)), ("zh", "zl", "core"), 0, 0)
    shape = (3, 2, 8, 256)
    return tuple(call(finish_kernel, [shape, shape], (parts, basis)))


def solution(mesh):
    fine = Mesh(mesh.devices.reshape(SIZES), AXES)
    inst, cell = ("y", "zh"), ("x", "zl", "core")
    out = P(None, cell, inst, None)
    return jax.shard_map(
        local,
        mesh=fine,
        in_specs=(
            P(inst, None, cell, None, None),
            P(inst, None, None, cell, None, None),
            P(cell, inst, None),
        ),
        out_specs=(out, out),
        check_vma=False,
    )
```

```python
import jax
import jax.numpy as jnp
import numpy as np
from jax import lax
from jax.experimental import pallas as pl
from jax.experimental.pallas import tpu as pltpu
from jax.sharding import Mesh, PartitionSpec as P

ITERS = 3
MU = 1.0
LAME = 1.5
AXES = ("y", "zh", "x", "zl", "core")
SIZES = (4, 2, 4, 4, 2)
F32 = jnp.float32


def flat(at):
    index = 0
    for size, k in zip(SIZES, at):
        index = index * size + k
    return index


def send(v, move):
    pairs = []
    for at in np.ndindex(*SIZES):
        to = move(*at)
        if to is not None:
            pairs.append((flat(at), flat(to)))
    return lax.ppermute(v, AXES, pairs)


def send_y(v, d):
    return send(v, lambda y, zh, x, zl, core: ((y + d) % 4, zh, x, zl, core))


def send_zh(v):
    return send(v, lambda y, zh, x, zl, core: (y, 1 - zh, x, zl, core))


def send_core(v):
    return send(v, lambda y, zh, x, zl, core: (y, zh, x, zl, 1 - core))


def send_pair(v):
    def move(y, zh, x, zl, core):
        q = x * 4 + zl + (1 if core == 1 else -1)
        return (y, zh, q // 4, q % 4, 1 - core) if 0 <= q < 16 else None

    return send(v, move)


VMEM = pl.BlockSpec(memory_space=pltpu.VMEM)


def call(kernel, outs, args, scratch=()):
    return pl.pallas_call(
        kernel,
        out_shape=[jax.ShapeDtypeStruct(s, F32) for s in outs],
        in_specs=[VMEM] * len(args),
        out_specs=[VMEM] * len(outs),
        scratch_shapes=list(scratch),
        compiler_params=pltpu.CompilerParams(vmem_limit_bytes=24 * 1024 * 1024),
    )(*args)


def sens_of_slab(slab, sign, f, a, got, wide):
    zero = jnp.zeros((8, 256), F32)
    for k in range(3):
        wide[k, 0:8, :] = zero
        wide[k, 64:72, :] = zero
    for rows in range(0, 64, 16):
        span = slice(rows, rows + 16)
        total = [None] * 3
        for i in range(2):
            for v in range(5):
                step = got[i, v, span, :].astype(F32) - a[i, v, span, :].astype(F32)
                for k in range(3):
                    term = f[i, v, k, slab, span, :].astype(F32) * step
                    total[k] = term if total[k] is None else total[k] + term
        for k in range(3):
            wide[k, rows + 3 : rows + 19, :] = total[k] * sign


def sens_early_kernel(f, a, got, wide):
    core = lax.axis_index("core")
    sens_of_slab(1 - core, jnp.where(core == 0, 1.0, -1.0), f, a, got, wide)


def sens_late_kernel(f, a, got, early, shift, m0, m1, m2, m3, wide):
    y, core = lax.axis_index("y"), lax.axis_index("core")
    sens_of_slab(core, jnp.where(core == 0, -1.0, 1.0), f, a, got, wide)
    for d, out in enumerate((m0, m1, m2, m3)):
        first = pl.multiple_of(lax.rem(y + d, 4) * 16, 16)
        for k in range(3):
            out[k * 3 : k * 3 + 3] = early[k, pl.ds(first, 24), :].reshape(3, 8, 256)
            out[9 + k * 3 : 12 + k * 3] = wide[k, pl.ds(first, 24), :].reshape(3, 8, 256)
    for out, span in ((m1, slice(6, 8)), (m2, slice(6, 8)), (m3, slice(0, 2))):
        for x in range(2):
            out[18, x * 2 : x * 2 + 2, :] = shift[x, span, :]
        out[18, 4:8, :] = jnp.zeros((4, 256), F32)


def sum_y_kernel(m0, r2, r1, r3, shift, own, out):
    zh = lax.axis_index("zh")
    for s in range(6):
        for g in range(2):
            for half, to in ((zh, own), (1 - zh, out)):
                k = s * 3 + half + g
                to[s * 2 + g] = (m0[k] + r1[k]) + (r2[k] + r3[k])
    low = zh == 0
    for x in range(2):
        below = jnp.where(low, shift[x, 6:8, :], r1[18, x * 2 : x * 2 + 2, :])
        above = jnp.where(low, r3[18, x * 2 : x * 2 + 2, :], shift[x, 0:2, :])
        out[12, x * 4 : x * 4 + 2, :] = below
        out[12, x * 4 + 2 : x * 4 + 4, :] = above


def krylov_kernel(block, mate, far, beyond, basis, moments, w0, w1, w2, sh):
    core = lax.axis_index("core")
    inst = lax.axis_index("y") * 2 + lax.axis_index("zh")
    cell = lax.axis_index("x") * 8 + lax.axis_index("zl") * 2 + core

    def place(x):
        return x + core * (7 - 2 * x)

    for k in range(3):
        line = (
            far[8 + k], far[k], far[3 + k], block[3 + k],
            block[k], mate[k], mate[3 + k], beyond[k],
        )
        for x in range(8):
            w0[k, place(x)] = line[x]
    for x in range(2):
        sh[1 + core * 4 + x] = far[6 + x]
        sh[3 + x] = block[6 + x]
        sh[5 - core * 4 + x] = mate[6 + x]

    row = lax.broadcasted_iota(jnp.int32, (16, 256), 0) + (inst * 8 - 3)
    lane = lax.broadcasted_iota(jnp.int32, (16, 256), 1)
    in_row = (row >= 0) & (row < 64)
    first, last = lane == 0, lane == 255

    def inside(x):
        at = cell * 2 - 3 + x
        return in_row & jnp.broadcast_to((at >= 0) & (at < 64), (16, 256))

    def y_up(v):
        return pltpu.roll(v, 15, 0)

    def y_down(v):
        return pltpu.roll(v, 1, 0)

    def z_up(v):
        return jnp.where(last, 0.0, pltpu.roll(v, 255, 1))

    def z_down(v):
        return jnp.where(first, 0.0, pltpu.roll(v, 1, 1))

    def apply(u, lo, hi, keep):
        before = None
        for x in range(lo - 1, hi + 1):
            c = [u(k, x) for k in range(3)]
            u1y, u2z = y_up(c[1]), z_up(c[2])
            dv = (u(0, x + 1) - c[0]) + (u1y - c[1]) + (u2z - c[2])
            mask = inside(x)
            dv = jnp.where(mask, dv, 0.0)
            if x >= lo:
                ups = [(y_up(c[0]), z_up(c[0])), (u1y, z_up(c[1])), (y_up(c[2]), u2z)]
                grads = [before, y_down(dv), z_down(dv)]
                weight = sh[x] + 6.0 * MU
                for k in range(3):
                    beside = (u(k, x + 1) + u(k, x - 1)) + (ups[k][0] + y_down(c[k]))
                    beside = beside + (ups[k][1] + z_down(c[k]))
                    image = weight * c[k] - MU * beside + LAME * (grads[k] - dv)
                    keep(k, x, jnp.where(mask, image, 0.0))
            before = dv

    def put(ref):
        def keep(k, x, v):
            ref[k, x] = v

        return keep

    apply(lambda k, x: w0[k, x], 1, 6, put(w1))
    apply(lambda k, x: w1[k, x], 2, 5, put(w2))
    sums = [None] * 6

    def finish(k, x, v):
        w = [w0[k, x, 3:11, :], w1[k, x, 3:11, :], w2[k, x, 3:11, :], v[3:11, :]]
        for j in range(4):
            basis[j, k, x - 3] = w[j]
        for n, (i, j) in enumerate(((0, 0), (0, 1), (1, 1), (1, 2), (2, 2), (2, 3))):
            term = w[i] * w[j]
            sums[n] = term if sums[n] is None else sums[n] + term

    apply(lambda k, x: w2[k, x], 3, 4, finish)
    moments[...] = jnp.zeros((8, 128), F32)
    for n in range(6):
        line = jnp.sum(sums[n], axis=0, keepdims=True)
        moments[n : n + 1, :] = line[:, :128] + line[:, 128:]


def two_sum(a, b):
    s = a + b
    t = s - a
    return s, (a - (s - t)) + (b - t)


def two_product(a, b):
    def halves(v):
        t = 4097.0 * v
        high = t - (t - v)
        return high, v - high

    p = a * b
    ah, al = halves(a)
    bh, bl = halves(b)
    return p, ((ah * bh - p) + ah * bl + al * bh) + al * bl


def finish_kernel(parts, basis, mesh_adjoint, residual):
    sums = [(parts[n], None) for n in range(parts.shape[0])]
    while len(sums) > 1:
        pairs = []
        for (p, rest), (q, more_rest) in zip(sums[::2], sums[1::2]):
            high, low = two_sum(p, q)
            pairs.append((high, low if rest is None else low + (rest + more_rest)))
        sums = pairs
    high, low = sums[0]
    for step in (64, 32, 16, 8, 4, 2, 1):
        high, error = two_sum(high, pltpu.roll(high, step, 1))
        low = (low + pltpu.roll(low, step, 1)) + error

    def line(v, n):
        return jnp.broadcast_to(v[n : n + 1, :], (8, 128))

    t = line(high, 1) / line(high, 0)
    centred = [line(high, 0) + line(low, 0)]
    for n in range(1, 6):
        product, error = two_product(t, high)
        error = error + t * low
        high, more = two_sum(pltpu.roll(high, 7, 0), -product)
        low = (pltpu.roll(low, 7, 0) - error) + more
        high, low = two_sum(high, low)
        centred.append(line(high, 0) + line(low, 0))

    def dot(u, v):
        total = None
        for i, p in enumerate(u):
            for j, q in enumerate(v):
                term = p * q * centred[i + j]
                total = term if total is None else total + term
        return total

    one = jnp.ones((8, 128), F32)
    r, p, x, now = [one], [one], [], centred[0]
    for sweep in range(ITERS):
        image = [t * p[0]] + [p[n - 1] + t * p[n] for n in range(1, len(p))] + [p[-1]]
        alpha = now / dot(p, image)
        x = [x[n] + alpha * p[n] if n < len(x) else alpha * p[n] for n in range(len(p))]
        r = [r[n] - alpha * image[n] if n < len(r) else -alpha * image[n] for n in range(len(image))]
        if sweep < ITERS - 1:
            new = dot(r, r)
            beta = new / now
            p = [r[n] + beta * p[n] if n < len(p) else r[n] for n in range(len(r))]
            now = new

    def monomials(c):
        out = [c[-1]]
        for term in c[-2::-1]:
            out = [term - t * out[0]] + [out[n - 1] - t * out[n] for n in range(1, len(out))] + [out[-1]]
        return [jnp.broadcast_to(v[0:1, 0:1], (8, 256)) for v in out]

    cx, cr = monomials(x), monomials(r)
    for k in range(3):
        for s in range(2):
            w = [basis[j, k, s] for j in range(4)]
            mesh_adjoint[k, s] = cx[0] * w[0] + cx[1] * w[1] + cx[2] * w[2]
            residual[k, s] = (cr[0] * w[0] + cr[1] * w[1]) + (cr[2] * w[2] + cr[3] * w[3])


def local(adjoint, flux_jac, shift):
    core = lax.axis_index("core")
    outer = lax.dynamic_index_in_dim(adjoint, core, 2, False)
    inner = lax.dynamic_index_in_dim(adjoint, 1 - core, 2, False)
    got_outer = send_pair(outer)
    got_inner = send_core(inner)

    rows = (3, 72, 256)
    (early,) = call(sens_early_kernel, [rows], (flux_jac, outer, got_inner))
    nineteen = (19, 8, 256)
    m0, m1, m2, m3 = call(
        sens_late_kernel,
        [(18, 8, 256)] + [nineteen] * 3,
        (flux_jac, inner, got_outer, early, shift),
        [pltpu.VMEM(rows, F32)],
    )
    r2, r1, r3 = send_y(m2, 2), send_y(m1, 1), send_y(m3, 3)
    own, out = call(sum_y_kernel, [(12, 8, 256), (13, 8, 256)], (m0, r2, r1, r3, shift))
    got = send_zh(out)
    sides = got[12].reshape(2, 4, 256)
    ends = [jnp.zeros((2, n, 256), F32) for n in (1, 3)]
    wider = jnp.concatenate([ends[0], sides[:, :2], shift, sides[:, 2:], ends[1]], axis=1)
    block = jnp.concatenate([(own + got[:12]).reshape(6, 16, 256), wider], axis=0)
    mate = send_core(block)
    far = send_pair(jnp.concatenate([block, mate[:3]], axis=0))
    beyond = send_core(far[3:6])

    scratch = pltpu.VMEM((3, 8, 16, 256), F32)
    basis, moments = call(
        krylov_kernel,
        [(4, 3, 2, 8, 256), (8, 128)],
        (block, mate, far, beyond),
        [scratch, scratch, scratch, pltpu.VMEM((8, 16, 256), F32)],
    )
    parts = lax.all_to_all(jnp.broadcast_to(moments, (16, 8, 128)), ("y", "x"), 0, 0)
    moments = jnp.sum(parts, axis=0)
    parts = lax.all_to_all(jnp.broadcast_to(moments, (16, 8, 128)), ("zh", "zl", "core"), 0, 0)
    shape = (3, 2, 8, 256)
    return tuple(call(finish_kernel, [shape, shape], (parts, basis)))


def solution(mesh):
    fine = Mesh(mesh.devices.reshape(SIZES), AXES)
    inst, cell = ("y", "zh"), ("x", "zl", "core")
    out = P(None, cell, inst, None)
    return jax.shard_map(
        local,
        mesh=fine,
        in_specs=(
            P(inst, None, cell, None, None),
            P(inst, None, None, cell, None, None),
            P(cell, inst, None),
        ),
        out_specs=(out, out),
        check_vma=False,
    )
```

```python
import jax
import jax.numpy as jnp
import numpy as np
from jax import lax
from jax.experimental import pallas as pl
from jax.experimental.pallas import tpu as pltpu
from jax.sharding import Mesh, PartitionSpec as P

ITERS = 3
MU = 1.0
LAME = 1.5
AXES = ("y", "zh", "x", "zl", "core")
SIZES = (4, 2, 4, 4, 2)
F32 = jnp.float32


def flat(at):
    index = 0
    for size, k in zip(SIZES, at):
        index = index * size + k
    return index


def send(v, move):
    pairs = []
    for at in np.ndindex(*SIZES):
        to = move(*at)
        if to is not None:
            pairs.append((flat(at), flat(to)))
    return lax.ppermute(v, AXES, pairs)


def send_y(v, d):
    return send(v, lambda y, zh, x, zl, core: ((y + d) % 4, zh, x, zl, core))


def send_zh(v):
    return send(v, lambda y, zh, x, zl, core: (y, 1 - zh, x, zl, core))


def send_core(v):
    return send(v, lambda y, zh, x, zl, core: (y, zh, x, zl, 1 - core))


def send_pair(v):
    def move(y, zh, x, zl, core):
        q = x * 4 + zl + (1 if core == 1 else -1)
        return (y, zh, q // 4, q % 4, 1 - core) if 0 <= q < 16 else None

    return send(v, move)


def send_chip(v):
    def move(y, zh, x, zl, core):
        q = x * 4 + zl + (1 if core == 0 else -1)
        return (y, zh, q // 4, q % 4, core) if 0 <= q < 16 else None

    return send(v, move)


VMEM = pl.BlockSpec(memory_space=pltpu.VMEM)


def call(kernel, outs, args, scratch=()):
    return pl.pallas_call(
        kernel,
        out_shape=[jax.ShapeDtypeStruct(s, F32) for s in outs],
        in_specs=[VMEM] * len(args),
        out_specs=[VMEM] * len(outs),
        scratch_shapes=list(scratch),
        compiler_params=pltpu.CompilerParams(vmem_limit_bytes=24 * 1024 * 1024),
    )(*args)


def sens_of_slab(slab, sign, f, a, got, wide):
    zero = jnp.zeros((8, 256), F32)
    for k in range(3):
        wide[k, 0:8, :] = zero
        wide[k, 64:72, :] = zero
    for rows in range(0, 64, 16):
        span = slice(rows, rows + 16)
        total = [None] * 3
        for i in range(2):
            for v in range(5):
                step = got[i, v, span, :].astype(F32) - a[i, v, span, :].astype(F32)
                for k in range(3):
                    term = f[i, v, k, slab, span, :].astype(F32) * step
                    total[k] = term if total[k] is None else total[k] + term
        for k in range(3):
            wide[k, rows + 3 : rows + 19, :] = total[k] * sign


def sens_early_kernel(f, a, got, wide):
    core = lax.axis_index("core")
    sens_of_slab(1 - core, jnp.where(core == 0, 1.0, -1.0), f, a, got, wide)


def sens_late_kernel(f, a, got, early, shift, m0, m1, m2, m3, wide):
    y, core = lax.axis_index("y"), lax.axis_index("core")
    sens_of_slab(core, jnp.where(core == 0, -1.0, 1.0), f, a, got, wide)
    for d, out in enumerate((m0, m1, m2, m3)):
        first = pl.multiple_of(lax.rem(y + d, 4) * 16, 16)
        for k in range(3):
            out[k * 3 : k * 3 + 3] = early[k, pl.ds(first, 24), :].reshape(3, 8, 256)
            out[9 + k * 3 : 12 + k * 3] = wide[k, pl.ds(first, 24), :].reshape(3, 8, 256)
    for out, span in ((m1, slice(6, 8)), (m2, slice(6, 8)), (m3, slice(0, 2))):
        for x in range(2):
            out[18, x * 2 : x * 2 + 2, :] = shift[x, span, :]
        out[18, 4:8, :] = jnp.zeros((4, 256), F32)


def sum_y_kernel(m0, r2, r1, r3, shift, own, out):
    zh = lax.axis_index("zh")
    for s in range(6):
        for g in range(2):
            for half, to in ((zh, own), (1 - zh, out)):
                k = s * 3 + half + g
                to[s * 2 + g] = (m0[k] + r1[k]) + (r2[k] + r3[k])
    low = zh == 0
    for x in range(2):
        below = jnp.where(low, shift[x, 6:8, :], r1[18, x * 2 : x * 2 + 2, :])
        above = jnp.where(low, r3[18, x * 2 : x * 2 + 2, :], shift[x, 0:2, :])
        out[12, x * 4 : x * 4 + 2, :] = below
        out[12, x * 4 + 2 : x * 4 + 4, :] = above


def krylov_kernel(block, mate, far, farther, beyond, basis, moments, w0, w1, w2, sh):
    core = lax.axis_index("core")
    inst = lax.axis_index("y") * 2 + lax.axis_index("zh")
    cell = lax.axis_index("x") * 8 + lax.axis_index("zl") * 2 + core

    def place(x):
        return x + core * (7 - 2 * x)

    for k in range(3):
        line = (
            farther[k], far[k], far[3 + k], block[3 + k],
            block[k], mate[k], mate[3 + k], beyond[k],
        )
        for x in range(8):
            w0[k, place(x)] = line[x]
    for x in range(2):
        sh[1 + core * 4 + x] = far[6 + x]
        sh[3 + x] = block[6 + x]
        sh[5 - core * 4 + x] = mate[6 + x]

    row = lax.broadcasted_iota(jnp.int32, (16, 256), 0) + (inst * 8 - 3)
    lane = lax.broadcasted_iota(jnp.int32, (16, 256), 1)
    in_row = (row >= 0) & (row < 64)
    first, last = lane == 0, lane == 255

    def inside(x):
        at = cell * 2 - 3 + x
        return in_row & jnp.broadcast_to((at >= 0) & (at < 64), (16, 256))

    def y_up(v):
        return pltpu.roll(v, 15, 0)

    def y_down(v):
        return pltpu.roll(v, 1, 0)

    def z_up(v):
        return jnp.where(last, 0.0, pltpu.roll(v, 255, 1))

    def z_down(v):
        return jnp.where(first, 0.0, pltpu.roll(v, 1, 1))

    def apply(u, lo, hi, keep):
        before = None
        for x in range(lo - 1, hi + 1):
            c = [u(k, x) for k in range(3)]
            u1y, u2z = y_up(c[1]), z_up(c[2])
            dv = (u(0, x + 1) - c[0]) + (u1y - c[1]) + (u2z - c[2])
            mask = inside(x)
            dv = jnp.where(mask, dv, 0.0)
            if x >= lo:
                ups = [(y_up(c[0]), z_up(c[0])), (u1y, z_up(c[1])), (y_up(c[2]), u2z)]
                grads = [before, y_down(dv), z_down(dv)]
                weight = sh[x] + 6.0 * MU
                for k in range(3):
                    beside = (u(k, x + 1) + u(k, x - 1)) + (ups[k][0] + y_down(c[k]))
                    beside = beside + (ups[k][1] + z_down(c[k]))
                    image = weight * c[k] - MU * beside + LAME * (grads[k] - dv)
                    keep(k, x, jnp.where(mask, image, 0.0))
            before = dv

    def put(ref):
        def keep(k, x, v):
            ref[k, x] = v

        return keep

    apply(lambda k, x: w0[k, x], 1, 6, put(w1))
    apply(lambda k, x: w1[k, x], 2, 5, put(w2))
    sums = [None] * 6

    def finish(k, x, v):
        w = [w0[k, x, 3:11, :], w1[k, x, 3:11, :], w2[k, x, 3:11, :], v[3:11, :]]
        for j in range(4):
            basis[j, k, x - 3] = w[j]
        for n, (i, j) in enumerate(((0, 0), (0, 1), (1, 1), (1, 2), (2, 2), (2, 3))):
            term = w[i] * w[j]
            sums[n] = term if sums[n] is None else sums[n] + term

    apply(lambda k, x: w2[k, x], 3, 4, finish)
    moments[...] = jnp.zeros((8, 128), F32)
    for n in range(6):
        line = jnp.sum(sums[n], axis=0, keepdims=True)
        moments[n : n + 1, :] = line[:, :128] + line[:, 128:]


def two_sum(a, b):
    s = a + b
    t = s - a
    return s, (a - (s - t)) + (b - t)


def two_product(a, b):
    def halves(v):
        t = 4097.0 * v
        high = t - (t - v)
        return high, v - high

    p = a * b
    ah, al = halves(a)
    bh, bl = halves(b)
    return p, ((ah * bh - p) + ah * bl + al * bh) + al * bl


def finish_kernel(parts, basis, mesh_adjoint, residual):
    sums = [(parts[n], None) for n in range(parts.shape[0])]
    while len(sums) > 1:
        pairs = []
        for (p, rest), (q, more_rest) in zip(sums[::2], sums[1::2]):
            high, low = two_sum(p, q)
            pairs.append((high, low if rest is None else low + (rest + more_rest)))
        sums = pairs
    high, low = sums[0]
    for step in (64, 32, 16, 8, 4, 2, 1):
        high, error = two_sum(high, pltpu.roll(high, step, 1))
        low = (low + pltpu.roll(low, step, 1)) + error

    def line(v, n):
        return jnp.broadcast_to(v[n : n + 1, :], (8, 128))

    t = line(high, 1) / line(high, 0)
    centred = [line(high, 0) + line(low, 0)]
    for n in range(1, 6):
        product, error = two_product(t, high)
        error = error + t * low
        high, more = two_sum(pltpu.roll(high, 7, 0), -product)
        low = (pltpu.roll(low, 7, 0) - error) + more
        high, low = two_sum(high, low)
        centred.append(line(high, 0) + line(low, 0))

    def dot(u, v):
        total = None
        for i, p in enumerate(u):
            for j, q in enumerate(v):
                term = p * q * centred[i + j]
                total = term if total is None else total + term
        return total

    one = jnp.ones((8, 128), F32)
    r, p, x, now = [one], [one], [], centred[0]
    for sweep in range(ITERS):
        image = [t * p[0]] + [p[n - 1] + t * p[n] for n in range(1, len(p))] + [p[-1]]
        alpha = now / dot(p, image)
        x = [x[n] + alpha * p[n] if n < len(x) else alpha * p[n] for n in range(len(p))]
        r = [r[n] - alpha * image[n] if n < len(r) else -alpha * image[n] for n in range(len(image))]
        if sweep < ITERS - 1:
            new = dot(r, r)
            beta = new / now
            p = [r[n] + beta * p[n] if n < len(p) else r[n] for n in range(len(r))]
            now = new

    def monomials(c):
        out = [c[-1]]
        for term in c[-2::-1]:
            out = [term - t * out[0]] + [out[n - 1] - t * out[n] for n in range(1, len(out))] + [out[-1]]
        return [jnp.broadcast_to(v[0:1, 0:1], (8, 256)) for v in out]

    cx, cr = monomials(x), monomials(r)
    for k in range(3):
        for s in range(2):
            w = [basis[j, k, s] for j in range(4)]
            mesh_adjoint[k, s] = cx[0] * w[0] + cx[1] * w[1] + cx[2] * w[2]
            residual[k, s] = (cr[0] * w[0] + cr[1] * w[1]) + (cr[2] * w[2] + cr[3] * w[3])


def local(adjoint, flux_jac, shift):
    core = lax.axis_index("core")
    outer = lax.dynamic_index_in_dim(adjoint, core, 2, False)
    inner = lax.dynamic_index_in_dim(adjoint, 1 - core, 2, False)
    got_outer = send_pair(outer)
    got_inner = send_core(inner)

    rows = (3, 72, 256)
    (early,) = call(sens_early_kernel, [rows], (flux_jac, outer, got_inner))
    nineteen = (19, 8, 256)
    m0, m1, m2, m3 = call(
        sens_late_kernel,
        [(18, 8, 256)] + [nineteen] * 3,
        (flux_jac, inner, got_outer, early, shift),
        [pltpu.VMEM(rows, F32)],
    )
    r2, r1, r3 = send_y(m2, 2), send_y(m1, 1), send_y(m3, 3)
    own, out = call(sum_y_kernel, [(12, 8, 256), (13, 8, 256)], (m0, r2, r1, r3, shift))
    got = send_zh(out)
    sides = got[12].reshape(2, 4, 256)
    ends = [jnp.zeros((2, n, 256), F32) for n in (1, 3)]
    wider = jnp.concatenate([ends[0], sides[:, :2], shift, sides[:, 2:], ends[1]], axis=1)
    block = jnp.concatenate([(own + got[:12]).reshape(6, 16, 256), wider], axis=0)
    far = send_pair(block)
    farther = send_chip(block[:3])
    mate = send_core(block)
    beyond = send_core(far[3:6])

    scratch = pltpu.VMEM((3, 8, 16, 256), F32)
    basis, moments = call(
        krylov_kernel,
        [(4, 3, 2, 8, 256), (8, 128)],
        (block, mate, far, farther, beyond),
        [scratch, scratch, scratch, pltpu.VMEM((8, 16, 256), F32)],
    )
    parts = lax.all_to_all(jnp.broadcast_to(moments, (16, 8, 128)), ("y", "x"), 0, 0)
    moments = jnp.sum(parts, axis=0)
    parts = lax.all_to_all(jnp.broadcast_to(moments, (16, 8, 128)), ("zh", "zl", "core"), 0, 0)
    shape = (3, 2, 8, 256)
    return tuple(call(finish_kernel, [shape, shape], (parts, basis)))


def solution(mesh):
    fine = Mesh(mesh.devices.reshape(SIZES), AXES)
    inst, cell = ("y", "zh"), ("x", "zl", "core")
    out = P(None, cell, inst, None)
    return jax.shard_map(
        local,
        mesh=fine,
        in_specs=(
            P(inst, None, cell, None, None),
            P(inst, None, None, cell, None, None),
            P(cell, inst, None),
        ),
        out_specs=(out, out),
        check_vma=False,
    )
```

```python
import jax
import jax.numpy as jnp
import numpy as np
from jax import lax
from jax.experimental import pallas as pl
from jax.experimental.pallas import tpu as pltpu
from jax.sharding import Mesh, PartitionSpec as P

ITERS = 3
MU = 1.0
LAME = 1.5
AXES = ("y", "zh", "x", "zl", "core")
SIZES = (4, 2, 4, 4, 2)
F32 = jnp.float32


def flat(at):
    index = 0
    for size, k in zip(SIZES, at):
        index = index * size + k
    return index


def send(v, move):
    pairs = []
    for at in np.ndindex(*SIZES):
        to = move(*at)
        if to is not None:
            pairs.append((flat(at), flat(to)))
    return lax.ppermute(v, AXES, pairs)


def send_y(v, d):
    return send(v, lambda y, zh, x, zl, core: ((y + d) % 4, zh, x, zl, core))


def send_zh(v):
    return send(v, lambda y, zh, x, zl, core: (y, 1 - zh, x, zl, core))


def send_core(v):
    return send(v, lambda y, zh, x, zl, core: (y, zh, x, zl, 1 - core))


def send_pair(v):
    def move(y, zh, x, zl, core):
        q = x * 4 + zl + (1 if core == 1 else -1)
        return (y, zh, q // 4, q % 4, 1 - core) if 0 <= q < 16 else None

    return send(v, move)


VMEM = pl.BlockSpec(memory_space=pltpu.VMEM)


def call(kernel, outs, args, scratch=()):
    return pl.pallas_call(
        kernel,
        out_shape=[jax.ShapeDtypeStruct(s, F32) for s in outs],
        in_specs=[VMEM] * len(args),
        out_specs=[VMEM] * len(outs),
        scratch_shapes=list(scratch),
        compiler_params=pltpu.CompilerParams(vmem_limit_bytes=24 * 1024 * 1024),
    )(*args)


def sens_of_slab(slab, sign, f, a, got, wide):
    zero = jnp.zeros((8, 256), F32)
    for k in range(3):
        wide[k, 0:8, :] = zero
        wide[k, 64:72, :] = zero
    for rows in range(0, 64, 16):
        span = slice(rows, rows + 16)
        total = [None] * 3
        for i in range(2):
            for v in range(5):
                step = got[i, v, span, :].astype(F32) - a[i, v, span, :].astype(F32)
                for k in range(3):
                    term = f[i, v, k, slab, span, :].astype(F32) * step
                    total[k] = term if total[k] is None else total[k] + term
        for k in range(3):
            wide[k, rows + 3 : rows + 19, :] = total[k] * sign


def cut(y, wide, outs):
    for d, out in enumerate(outs):
        first = pl.multiple_of(lax.rem(y + d, 4) * 16, 16)
        for k in range(3):
            out[k * 3 : k * 3 + 3] = wide[k, pl.ds(first, 24), :].reshape(3, 8, 256)


def sens_early_kernel(f, a, got, shift, m0, m1, m2, m3, wide):
    core = lax.axis_index("core")
    sens_of_slab(1 - core, jnp.where(core == 0, 1.0, -1.0), f, a, got, wide)
    cut(lax.axis_index("y"), wide, (m0, m1, m2, m3))
    for out, span in ((m1, slice(6, 8)), (m2, slice(6, 8)), (m3, slice(0, 2))):
        for x in range(2):
            out[9, x * 2 : x * 2 + 2, :] = shift[x, span, :]
        out[9, 4:8, :] = jnp.zeros((4, 256), F32)


def sens_late_kernel(f, a, got, after, m0, m1, m2, m3, wide):
    core = lax.axis_index("core")
    sens_of_slab(core, jnp.where(core == 0, -1.0, 1.0), f, a, got, wide)
    cut(lax.axis_index("y"), wide, (m0, m1, m2, m3))


def sum_y(m0, r2, r1, r3, own, out):
    zh = lax.axis_index("zh")
    for s in range(3):
        for g in range(2):
            for half, to in ((zh, own), (1 - zh, out)):
                k = s * 3 + half + g
                to[s * 2 + g] = (m0[k] + r1[k]) + (r2[k] + r3[k])


def sum_y_early_kernel(m0, r2, r1, r3, shift, after, own, out):
    sum_y(m0, r2, r1, r3, own, out)
    low = lax.axis_index("zh") == 0
    for x in range(2):
        below = jnp.where(low, shift[x, 6:8, :], r1[9, x * 2 : x * 2 + 2, :])
        above = jnp.where(low, r3[9, x * 2 : x * 2 + 2, :], shift[x, 0:2, :])
        out[6, x * 4 : x * 4 + 2, :] = below
        out[6, x * 4 + 2 : x * 4 + 4, :] = above


def sum_y_late_kernel(m0, r2, r1, r3, own_early, out_early, own, out):
    sum_y(m0, r2, r1, r3, own, out)
    own[6:12] = own_early[...]
    out[6:13] = out_early[...]


def krylov_kernel(block, mate, far, beyond, basis, moments, w0, w1, w2, sh):
    core = lax.axis_index("core")
    inst = lax.axis_index("y") * 2 + lax.axis_index("zh")
    cell = lax.axis_index("x") * 8 + lax.axis_index("zl") * 2 + core

    def place(x):
        return x + core * (7 - 2 * x)

    for k in range(3):
        line = (
            far[8 + k], far[3 + k], far[k], block[k],
            block[3 + k], mate[3 + k], mate[k], beyond[k],
        )
        for x in range(8):
            w0[k, place(x)] = line[x]
    for x in range(2):
        sh[1 + core * 4 + x] = far[6 + x]
        sh[3 + x] = block[6 + x]
        sh[5 - core * 4 + x] = mate[6 + x]

    row = lax.broadcasted_iota(jnp.int32, (16, 256), 0) + (inst * 8 - 3)
    lane = lax.broadcasted_iota(jnp.int32, (16, 256), 1)
    in_row = (row >= 0) & (row < 64)
    first, last = lane == 0, lane == 255

    def inside(x):
        at = cell * 2 - 3 + x
        return in_row & jnp.broadcast_to((at >= 0) & (at < 64), (16, 256))

    def y_up(v):
        return pltpu.roll(v, 15, 0)

    def y_down(v):
        return pltpu.roll(v, 1, 0)

    def z_up(v):
        return jnp.where(last, 0.0, pltpu.roll(v, 255, 1))

    def z_down(v):
        return jnp.where(first, 0.0, pltpu.roll(v, 1, 1))

    def apply(u, lo, hi, keep):
        before = None
        for x in range(lo - 1, hi + 1):
            c = [u(k, x) for k in range(3)]
            u1y, u2z = y_up(c[1]), z_up(c[2])
            dv = (u(0, x + 1) - c[0]) + (u1y - c[1]) + (u2z - c[2])
            mask = inside(x)
            dv = jnp.where(mask, dv, 0.0)
            if x >= lo:
                ups = [(y_up(c[0]), z_up(c[0])), (u1y, z_up(c[1])), (y_up(c[2]), u2z)]
                grads = [before, y_down(dv), z_down(dv)]
                weight = sh[x] + 6.0 * MU
                for k in range(3):
                    beside = (u(k, x + 1) + u(k, x - 1)) + (ups[k][0] + y_down(c[k]))
                    beside = beside + (ups[k][1] + z_down(c[k]))
                    image = weight * c[k] - MU * beside + LAME * (grads[k] - dv)
                    keep(k, x, jnp.where(mask, image, 0.0))
            before = dv

    def put(ref):
        def keep(k, x, v):
            ref[k, x] = v

        return keep

    apply(lambda k, x: w0[k, x], 1, 6, put(w1))
    apply(lambda k, x: w1[k, x], 2, 5, put(w2))
    sums = [None] * 6

    def finish(k, x, v):
        w = [w0[k, x, 3:11, :], w1[k, x, 3:11, :], w2[k, x, 3:11, :], v[3:11, :]]
        for j in range(4):
            basis[j, k, x - 3] = w[j]
        for n, (i, j) in enumerate(((0, 0), (0, 1), (1, 1), (1, 2), (2, 2), (2, 3))):
            term = w[i] * w[j]
            sums[n] = term if sums[n] is None else sums[n] + term

    apply(lambda k, x: w2[k, x], 3, 4, finish)
    moments[...] = jnp.zeros((8, 128), F32)
    for n in range(6):
        line = jnp.sum(sums[n], axis=0, keepdims=True)
        moments[n : n + 1, :] = line[:, :128] + line[:, 128:]


def two_sum(a, b):
    s = a + b
    t = s - a
    return s, (a - (s - t)) + (b - t)


def two_product(a, b):
    def halves(v):
        t = 4097.0 * v
        high = t - (t - v)
        return high, v - high

    p = a * b
    ah, al = halves(a)
    bh, bl = halves(b)
    return p, ((ah * bh - p) + ah * bl + al * bh) + al * bl


def finish_kernel(parts, basis, mesh_adjoint, residual):
    sums = [(parts[n], None) for n in range(parts.shape[0])]
    while len(sums) > 1:
        pairs = []
        for (p, rest), (q, more_rest) in zip(sums[::2], sums[1::2]):
            high, low = two_sum(p, q)
            pairs.append((high, low if rest is None else low + (rest + more_rest)))
        sums = pairs
    high, low = sums[0]
    for step in (64, 32, 16, 8, 4, 2, 1):
        high, error = two_sum(high, pltpu.roll(high, step, 1))
        low = (low + pltpu.roll(low, step, 1)) + error

    def line(v, n):
        return jnp.broadcast_to(v[n : n + 1, :], (8, 128))

    t = line(high, 1) / line(high, 0)
    centred = [line(high, 0) + line(low, 0)]
    for n in range(1, 6):
        product, error = two_product(t, high)
        error = error + t * low
        high, more = two_sum(pltpu.roll(high, 7, 0), -product)
        low = (pltpu.roll(low, 7, 0) - error) + more
        high, low = two_sum(high, low)
        centred.append(line(high, 0) + line(low, 0))

    def dot(u, v):
        total = None
        for i, p in enumerate(u):
            for j, q in enumerate(v):
                term = p * q * centred[i + j]
                total = term if total is None else total + term
        return total

    one = jnp.ones((8, 128), F32)
    r, p, x, now = [one], [one], [], centred[0]
    for sweep in range(ITERS):
        image = [t * p[0]] + [p[n - 1] + t * p[n] for n in range(1, len(p))] + [p[-1]]
        alpha = now / dot(p, image)
        x = [x[n] + alpha * p[n] if n < len(x) else alpha * p[n] for n in range(len(p))]
        r = [r[n] - alpha * image[n] if n < len(r) else -alpha * image[n] for n in range(len(image))]
        if sweep < ITERS - 1:
            new = dot(r, r)
            beta = new / now
            p = [r[n] + beta * p[n] if n < len(p) else r[n] for n in range(len(r))]
            now = new

    def monomials(c):
        out = [c[-1]]
        for term in c[-2::-1]:
            out = [term - t * out[0]] + [out[n - 1] - t * out[n] for n in range(1, len(out))] + [out[-1]]
        return [jnp.broadcast_to(v[0:1, 0:1], (8, 256)) for v in out]

    cx, cr = monomials(x), monomials(r)
    for k in range(3):
        for s in range(2):
            w = [basis[j, k, s] for j in range(4)]
            mesh_adjoint[k, s] = cx[0] * w[0] + cx[1] * w[1] + cx[2] * w[2]
            residual[k, s] = (cr[0] * w[0] + cr[1] * w[1]) + (cr[2] * w[2] + cr[3] * w[3])


def local(adjoint, flux_jac, shift):
    core = lax.axis_index("core")
    outer = lax.dynamic_index_in_dim(adjoint, core, 2, False)
    inner = lax.dynamic_index_in_dim(adjoint, 1 - core, 2, False)
    got_outer = send_pair(outer)
    got_inner = send_core(inner)

    six, nine, ten = (6, 8, 256), (9, 8, 256), (10, 8, 256)
    wide = [pltpu.VMEM((3, 72, 256), F32)]
    m0, m1, m2, m3 = call(
        sens_early_kernel, [nine, ten, ten, ten], (flux_jac, outer, got_inner, shift), wide
    )
    r2, r1, r3 = send_y(m2, 2), send_y(m1, 1), send_y(m3, 3)
    n0, n1, n2, n3 = call(sens_late_kernel, [nine] * 4, (flux_jac, inner, got_outer, m0), wide)
    q2, q1, q3 = send_y(n2, 2), send_y(n1, 1), send_y(n3, 3)
    own, out = call(sum_y_early_kernel, [six, (7, 8, 256)], (m0, r2, r1, r3, shift, n0))
    own, out = call(sum_y_late_kernel, [(12, 8, 256), (13, 8, 256)], (n0, q2, q1, q3, own, out))
    got = send_zh(out)
    sides = got[12].reshape(2, 4, 256)
    ends = [jnp.zeros((2, n, 256), F32) for n in (1, 3)]
    wider = jnp.concatenate([ends[0], sides[:, :2], shift, sides[:, 2:], ends[1]], axis=1)
    block = jnp.concatenate([(own + got[:12]).reshape(6, 16, 256), wider], axis=0)
    mate = send_core(block)
    far = send_pair(jnp.concatenate([block, mate[3:6]], axis=0))
    beyond = send_core(far[:3])

    scratch = pltpu.VMEM((3, 8, 16, 256), F32)
    basis, moments = call(
        krylov_kernel,
        [(4, 3, 2, 8, 256), (8, 128)],
        (block, mate, far, beyond),
        [scratch, scratch, scratch, pltpu.VMEM((8, 16, 256), F32)],
    )
    parts = lax.all_to_all(jnp.broadcast_to(moments, (16, 8, 128)), ("zh", "zl", "core"), 0, 0)
    moments = jnp.sum(parts, axis=0)
    parts = lax.all_to_all(jnp.broadcast_to(moments, (16, 8, 128)), ("y", "x"), 0, 0)
    shape = (3, 2, 8, 256)
    return tuple(call(finish_kernel, [shape, shape], (parts, basis)))


def solution(mesh):
    fine = Mesh(mesh.devices.reshape(SIZES), AXES)
    inst, cell = ("y", "zh"), ("x", "zl", "core")
    out = P(None, cell, inst, None)
    return jax.shard_map(
        local,
        mesh=fine,
        in_specs=(
            P(inst, None, cell, None, None),
            P(inst, None, None, cell, None, None),
            P(cell, inst, None),
        ),
        out_specs=(out, out),
        check_vma=False,
    )
```

```python
import jax
import jax.numpy as jnp
import numpy as np
from jax import lax
from jax.experimental import pallas as pl
from jax.experimental.pallas import tpu as pltpu
from jax.sharding import Mesh, PartitionSpec as P

ITERS = 3
MU = 1.0
LAME = 1.5
AXES = ("y", "zh", "x", "zl", "core")
SIZES = (4, 2, 4, 4, 2)
F32 = jnp.float32


def flat(at):
    index = 0
    for size, k in zip(SIZES, at):
        index = index * size + k
    return index


def send(v, move):
    pairs = []
    for at in np.ndindex(*SIZES):
        to = move(*at)
        if to is not None:
            pairs.append((flat(at), flat(to)))
    return lax.ppermute(v, AXES, pairs)


def send_y(v, d):
    return send(v, lambda y, zh, x, zl, core: ((y + d) % 4, zh, x, zl, core))


def send_zh(v):
    return send(v, lambda y, zh, x, zl, core: (y, 1 - zh, x, zl, core))


def send_core(v):
    return send(v, lambda y, zh, x, zl, core: (y, zh, x, zl, 1 - core))


def send_pair(v):
    def move(y, zh, x, zl, core):
        q = x * 4 + zl + (1 if core == 1 else -1)
        return (y, zh, q // 4, q % 4, 1 - core) if 0 <= q < 16 else None

    return send(v, move)


VMEM = pl.BlockSpec(memory_space=pltpu.VMEM)


def call(kernel, outs, args, scratch=()):
    return pl.pallas_call(
        kernel,
        out_shape=[jax.ShapeDtypeStruct(s, F32) for s in outs],
        in_specs=[VMEM] * len(args),
        out_specs=[VMEM] * len(outs),
        scratch_shapes=list(scratch),
        compiler_params=pltpu.CompilerParams(vmem_limit_bytes=24 * 1024 * 1024),
    )(*args)


def sens_of_slab(slab, sign, f, a, got, wide):
    zero = jnp.zeros((8, 256), F32)
    for k in range(3):
        wide[k, 0:8, :] = zero
        wide[k, 64:72, :] = zero
    for rows in range(0, 64, 16):
        span = slice(rows, rows + 16)
        total = [None] * 3
        for i in range(2):
            for v in range(5):
                step = got[i, v, span, :].astype(F32) - a[i, v, span, :].astype(F32)
                for k in range(3):
                    term = f[i, v, k, slab, span, :].astype(F32) * step
                    total[k] = term if total[k] is None else total[k] + term
        for k in range(3):
            wide[k, rows + 3 : rows + 19, :] = total[k] * sign


def cut(y, wide, outs):
    for d, out in enumerate(outs):
        first = pl.multiple_of(lax.rem(y + d, 4) * 16, 16)
        for k in range(3):
            out[k * 3 : k * 3 + 3] = wide[k, pl.ds(first, 24), :].reshape(3, 8, 256)


def sens_early_kernel(f, a, got, shift, m0, m1, m2, m3, wide):
    core = lax.axis_index("core")
    sens_of_slab(1 - core, jnp.where(core == 0, 1.0, -1.0), f, a, got, wide)
    cut(lax.axis_index("y"), wide, (m0, m1, m2, m3))
    for out, span in ((m1, slice(6, 8)), (m2, slice(6, 8)), (m3, slice(0, 2))):
        for x in range(2):
            out[9, x * 2 : x * 2 + 2, :] = shift[x, span, :]
        out[9, 4:8, :] = jnp.zeros((4, 256), F32)


def sens_late_kernel(f, a, got, after, m0, m1, m2, m3, wide):
    core = lax.axis_index("core")
    sens_of_slab(core, jnp.where(core == 0, -1.0, 1.0), f, a, got, wide)
    cut(lax.axis_index("y"), wide, (m0, m1, m2, m3))


def sum_y(m0, r2, r1, r3, own, out):
    zh = lax.axis_index("zh")
    for s in range(3):
        for g in range(2):
            for half, to in ((zh, own), (1 - zh, out)):
                k = s * 3 + half + g
                to[s * 2 + g] = (m0[k] + r1[k]) + (r2[k] + r3[k])


def sum_y_early_kernel(m0, r2, r1, r3, shift, after, own, out):
    sum_y(m0, r2, r1, r3, own, out)
    low = lax.axis_index("zh") == 0
    for x in range(2):
        below = jnp.where(low, shift[x, 6:8, :], r1[9, x * 2 : x * 2 + 2, :])
        above = jnp.where(low, r3[9, x * 2 : x * 2 + 2, :], shift[x, 0:2, :])
        out[6, x * 4 : x * 4 + 2, :] = below
        out[6, x * 4 + 2 : x * 4 + 4, :] = above


def sum_y_late_kernel(m0, r2, r1, r3, own_early, out_early, own, out):
    sum_y(m0, r2, r1, r3, own, out)
    own[6:12] = own_early[...]
    out[6:13] = out_early[...]


def krylov_kernel(block, mate, far, beyond, basis, moments, w0, w1, w2, sh):
    core = lax.axis_index("core")
    inst = lax.axis_index("y") * 2 + lax.axis_index("zh")
    cell = lax.axis_index("x") * 8 + lax.axis_index("zl") * 2 + core

    def place(x):
        return x + core * (7 - 2 * x)

    for k in range(3):
        line = (
            far[8 + k], far[3 + k], far[k], block[k],
            block[3 + k], mate[3 + k], mate[k], beyond[k],
        )
        for x in range(8):
            w0[k, place(x)] = line[x]
    for x in range(2):
        sh[1 + core * 4 + x] = far[6 + x]
        sh[3 + x] = block[6 + x]
        sh[5 - core * 4 + x] = mate[6 + x]

    row = lax.broadcasted_iota(jnp.int32, (16, 256), 0) + (inst * 8 - 3)
    lane = lax.broadcasted_iota(jnp.int32, (16, 256), 1)
    in_row = (row >= 0) & (row < 64)
    first, last = lane == 0, lane == 255

    def inside(x):
        at = cell * 2 - 3 + x
        return in_row & jnp.broadcast_to((at >= 0) & (at < 64), (16, 256))

    def y_up(v):
        return pltpu.roll(v, 15, 0)

    def y_down(v):
        return pltpu.roll(v, 1, 0)

    def z_up(v):
        return jnp.where(last, 0.0, pltpu.roll(v, 255, 1))

    def z_down(v):
        return jnp.where(first, 0.0, pltpu.roll(v, 1, 1))

    def apply(u, lo, hi, keep):
        before = None
        for x in range(lo - 1, hi + 1):
            c = [u(k, x) for k in range(3)]
            u1y, u2z = y_up(c[1]), z_up(c[2])
            dv = (u(0, x + 1) - c[0]) + (u1y - c[1]) + (u2z - c[2])
            mask = inside(x)
            dv = jnp.where(mask, dv, 0.0)
            if x >= lo:
                ups = [(y_up(c[0]), z_up(c[0])), (u1y, z_up(c[1])), (y_up(c[2]), u2z)]
                grads = [before, y_down(dv), z_down(dv)]
                weight = sh[x] + 6.0 * MU
                for k in range(3):
                    beside = (u(k, x + 1) + u(k, x - 1)) + (ups[k][0] + y_down(c[k]))
                    beside = beside + (ups[k][1] + z_down(c[k]))
                    image = weight * c[k] - MU * beside + LAME * (grads[k] - dv)
                    keep(k, x, jnp.where(mask, image, 0.0))
            before = dv

    def put(ref):
        def keep(k, x, v):
            ref[k, x] = v

        return keep

    apply(lambda k, x: w0[k, x], 1, 6, put(w1))
    apply(lambda k, x: w1[k, x], 2, 5, put(w2))
    sums = [None] * 6

    def finish(k, x, v):
        w = [w0[k, x, 3:11, :], w1[k, x, 3:11, :], w2[k, x, 3:11, :], v[3:11, :]]
        for j in range(4):
            basis[j, k, x - 3] = w[j]
        for n, (i, j) in enumerate(((0, 0), (0, 1), (1, 1), (1, 2), (2, 2), (2, 3))):
            term = w[i] * w[j]
            sums[n] = term if sums[n] is None else sums[n] + term

    apply(lambda k, x: w2[k, x], 3, 4, finish)
    moments[...] = jnp.zeros((8, 128), F32)
    for n in range(6):
        line = jnp.sum(sums[n], axis=0, keepdims=True)
        moments[n : n + 1, :] = line[:, :128] + line[:, 128:]


def two_sum(a, b):
    s = a + b
    t = s - a
    return s, (a - (s - t)) + (b - t)


def two_product(a, b):
    def halves(v):
        t = 4097.0 * v
        high = t - (t - v)
        return high, v - high

    p = a * b
    ah, al = halves(a)
    bh, bl = halves(b)
    return p, ((ah * bh - p) + ah * bl + al * bh) + al * bl


def finish_kernel(parts, basis, mesh_adjoint, residual):
    sums = [(parts[n], None) for n in range(parts.shape[0])]
    while len(sums) > 1:
        pairs = []
        for (p, rest), (q, more_rest) in zip(sums[::2], sums[1::2]):
            high, low = two_sum(p, q)
            pairs.append((high, low if rest is None else low + (rest + more_rest)))
        sums = pairs
    high, low = sums[0]
    cut = 4096.0 * jnp.max(jnp.abs(high), axis=1, keepdims=True)
    lead = (high + cut) - cut
    rest = jnp.sum((high - lead) + low, axis=1, keepdims=True)
    high, low = two_sum(jnp.sum(lead, axis=1, keepdims=True), rest)
    high, low = jnp.broadcast_to(high, (8, 128)), jnp.broadcast_to(low, (8, 128))

    def line(v, n):
        return jnp.broadcast_to(v[n : n + 1, :], (8, 128))

    t = line(high, 1) / line(high, 0)
    centred = [line(high, 0) + line(low, 0)]
    for n in range(1, 6):
        product, error = two_product(t, high)
        error = error + t * low
        high, more = two_sum(pltpu.roll(high, 7, 0), -product)
        low = (pltpu.roll(low, 7, 0) - error) + more
        high, low = two_sum(high, low)
        centred.append(line(high, 0) + line(low, 0))

    def dot(u, v):
        total = None
        for i, p in enumerate(u):
            for j, q in enumerate(v):
                term = p * q * centred[i + j]
                total = term if total is None else total + term
        return total

    one = jnp.ones((8, 128), F32)
    r, p, x, now = [one], [one], [], centred[0]
    for sweep in range(ITERS):
        image = [t * p[0]] + [p[n - 1] + t * p[n] for n in range(1, len(p))] + [p[-1]]
        alpha = now / dot(p, image)
        x = [x[n] + alpha * p[n] if n < len(x) else alpha * p[n] for n in range(len(p))]
        r = [r[n] - alpha * image[n] if n < len(r) else -alpha * image[n] for n in range(len(image))]
        if sweep < ITERS - 1:
            new = dot(r, r)
            beta = new / now
            p = [r[n] + beta * p[n] if n < len(p) else r[n] for n in range(len(r))]
            now = new

    def monomials(c):
        out = [c[-1]]
        for term in c[-2::-1]:
            out = [term - t * out[0]] + [out[n - 1] - t * out[n] for n in range(1, len(out))] + [out[-1]]
        return [jnp.broadcast_to(v[0:1, 0:1], (8, 256)) for v in out]

    cx, cr = monomials(x), monomials(r)
    for k in range(3):
        for s in range(2):
            w = [basis[j, k, s] for j in range(4)]
            mesh_adjoint[k, s] = cx[0] * w[0] + cx[1] * w[1] + cx[2] * w[2]
            residual[k, s] = (cr[0] * w[0] + cr[1] * w[1]) + (cr[2] * w[2] + cr[3] * w[3])


def local(adjoint, flux_jac, shift):
    core = lax.axis_index("core")
    outer = lax.dynamic_index_in_dim(adjoint, core, 2, False)
    inner = lax.dynamic_index_in_dim(adjoint, 1 - core, 2, False)
    got_outer = send_pair(outer)
    got_inner = send_core(inner)

    six, nine, ten = (6, 8, 256), (9, 8, 256), (10, 8, 256)
    wide = [pltpu.VMEM((3, 72, 256), F32)]
    m0, m1, m2, m3 = call(
        sens_early_kernel, [nine, ten, ten, ten], (flux_jac, outer, got_inner, shift), wide
    )
    r2, r1, r3 = send_y(m2, 2), send_y(m1, 1), send_y(m3, 3)
    n0, n1, n2, n3 = call(sens_late_kernel, [nine] * 4, (flux_jac, inner, got_outer, m0), wide)
    q2, q1, q3 = send_y(n2, 2), send_y(n1, 1), send_y(n3, 3)
    own, out = call(sum_y_early_kernel, [six, (7, 8, 256)], (m0, r2, r1, r3, shift, n0))
    own, out = call(sum_y_late_kernel, [(12, 8, 256), (13, 8, 256)], (n0, q2, q1, q3, own, out))
    got = send_zh(out)
    sides = got[12].reshape(2, 4, 256)
    ends = [jnp.zeros((2, n, 256), F32) for n in (1, 3)]
    wider = jnp.concatenate([ends[0], sides[:, :2], shift, sides[:, 2:], ends[1]], axis=1)
    block = jnp.concatenate([(own + got[:12]).reshape(6, 16, 256), wider], axis=0)
    mate = send_core(block)
    far = send_pair(jnp.concatenate([block, mate[3:6]], axis=0))
    beyond = send_core(far[:3])

    scratch = pltpu.VMEM((3, 8, 16, 256), F32)
    basis, moments = call(
        krylov_kernel,
        [(4, 3, 2, 8, 256), (8, 128)],
        (block, mate, far, beyond),
        [scratch, scratch, scratch, pltpu.VMEM((8, 16, 256), F32)],
    )
    parts = lax.all_to_all(jnp.broadcast_to(moments, (16, 8, 128)), ("zh", "zl", "core"), 0, 0)
    moments = jnp.sum(parts, axis=0)
    parts = lax.all_to_all(jnp.broadcast_to(moments, (16, 8, 128)), ("y", "x"), 0, 0)
    shape = (3, 2, 8, 256)
    return tuple(call(finish_kernel, [shape, shape], (parts, basis)))


def solution(mesh):
    fine = Mesh(mesh.devices.reshape(SIZES), AXES)
    inst, cell = ("y", "zh"), ("x", "zl", "core")
    out = P(None, cell, inst, None)
    return jax.shard_map(
        local,
        mesh=fine,
        in_specs=(
            P(inst, None, cell, None, None),
            P(inst, None, None, cell, None, None),
            P(cell, inst, None),
        ),
        out_specs=(out, out),
        check_vma=False,
    )
```

```python
import jax
import jax.numpy as jnp
import numpy as np
from jax import lax
from jax.experimental import pallas as pl
from jax.experimental.pallas import tpu as pltpu
from jax.sharding import Mesh, PartitionSpec as P

ITERS = 3
MU = 1.0
LAME = 1.5
AXES = ("y", "zh", "x", "zl", "core")
SIZES = (4, 2, 4, 4, 2)
F32 = jnp.float32


def flat(at):
    index = 0
    for size, k in zip(SIZES, at):
        index = index * size + k
    return index


def send(v, move):
    pairs = []
    for at in np.ndindex(*SIZES):
        to = move(*at)
        if to is not None:
            pairs.append((flat(at), flat(to)))
    return lax.ppermute(v, AXES, pairs)


def send_y(v, d):
    return send(v, lambda y, zh, x, zl, core: ((y + d) % 4, zh, x, zl, core))


def send_zh(v):
    return send(v, lambda y, zh, x, zl, core: (y, 1 - zh, x, zl, core))


def send_core(v):
    return send(v, lambda y, zh, x, zl, core: (y, zh, x, zl, 1 - core))


def send_pair(v):
    def move(y, zh, x, zl, core):
        q = x * 4 + zl + (1 if core == 1 else -1)
        return (y, zh, q // 4, q % 4, 1 - core) if 0 <= q < 16 else None

    return send(v, move)


VMEM = pl.BlockSpec(memory_space=pltpu.VMEM)


def call(kernel, outs, args, scratch=()):
    return pl.pallas_call(
        kernel,
        out_shape=[jax.ShapeDtypeStruct(s, F32) for s in outs],
        in_specs=[VMEM] * len(args),
        out_specs=[VMEM] * len(outs),
        scratch_shapes=list(scratch),
        compiler_params=pltpu.CompilerParams(vmem_limit_bytes=24 * 1024 * 1024),
    )(*args)


def sens_of_slab(slab, sign, f, a, got, wide):
    zero = jnp.zeros((8, 256), F32)
    for k in range(3):
        wide[k, 0:8, :] = zero
        wide[k, 64:72, :] = zero
    for rows in range(0, 64, 16):
        span = slice(rows, rows + 16)
        total = [None] * 3
        for i in range(2):
            for v in range(5):
                step = got[i, v, span, :].astype(F32) - a[i, v, span, :].astype(F32)
                for k in range(3):
                    term = f[i, v, k, slab, span, :].astype(F32) * step
                    total[k] = term if total[k] is None else total[k] + term
        for k in range(3):
            wide[k, rows + 3 : rows + 19, :] = total[k] * sign


def cut(y, wide, outs):
    for d, out in enumerate(outs):
        first = pl.multiple_of(lax.rem(y + d, 4) * 16, 16)
        for k in range(3):
            out[k * 3 : k * 3 + 3] = wide[k, pl.ds(first, 24), :].reshape(3, 8, 256)


def sens_early_kernel(f, a, got, shift, m0, m1, m2, m3, wide):
    core = lax.axis_index("core")
    sens_of_slab(1 - core, jnp.where(core == 0, 1.0, -1.0), f, a, got, wide)
    cut(lax.axis_index("y"), wide, (m0, m1, m2, m3))
    for out, span in ((m1, slice(6, 8)), (m2, slice(6, 8)), (m3, slice(0, 2))):
        for x in range(2):
            out[9, x * 2 : x * 2 + 2, :] = shift[x, span, :]
        out[9, 4:8, :] = jnp.zeros((4, 256), F32)


def sens_late_kernel(f, a, got, after, m0, m1, m2, m3, wide):
    core = lax.axis_index("core")
    sens_of_slab(core, jnp.where(core == 0, -1.0, 1.0), f, a, got, wide)
    cut(lax.axis_index("y"), wide, (m0, m1, m2, m3))


def sum_y(m0, r2, r1, r3, own, out):
    zh = lax.axis_index("zh")
    for s in range(3):
        for g in range(2):
            for half, to in ((zh, own), (1 - zh, out)):
                k = s * 3 + half + g
                to[s * 2 + g] = (m0[k] + r1[k]) + (r2[k] + r3[k])


def sum_y_early_kernel(m0, r1, r3, r2, shift, after, own, out):
    sum_y(m0, r2, r1, r3, own, out)
    low = lax.axis_index("zh") == 0
    for x in range(2):
        below = jnp.where(low, shift[x, 6:8, :], r1[9, x * 2 : x * 2 + 2, :])
        above = jnp.where(low, r3[9, x * 2 : x * 2 + 2, :], shift[x, 0:2, :])
        out[6, x * 4 : x * 4 + 2, :] = below
        out[6, x * 4 + 2 : x * 4 + 4, :] = above


def sum_y_late_kernel(m0, r1, r3, r2, own_early, out_early, own, out):
    sum_y(m0, r2, r1, r3, own, out)
    own[6:12] = own_early[...]
    out[6:13] = out_early[...]


def krylov_kernel(block, mate, far, beyond, basis, moments, w0, w1, w2, sh):
    core = lax.axis_index("core")
    inst = lax.axis_index("y") * 2 + lax.axis_index("zh")
    cell = lax.axis_index("x") * 8 + lax.axis_index("zl") * 2 + core

    def place(x):
        return x + core * (7 - 2 * x)

    for k in range(3):
        line = (
            far[8 + k], far[3 + k], far[k], block[k],
            block[3 + k], mate[3 + k], mate[k], beyond[k],
        )
        for x in range(8):
            w0[k, place(x)] = line[x]
    for x in range(2):
        sh[1 + core * 4 + x] = far[6 + x]
        sh[3 + x] = block[6 + x]
        sh[5 - core * 4 + x] = mate[6 + x]

    row = lax.broadcasted_iota(jnp.int32, (16, 256), 0) + (inst * 8 - 3)
    lane = lax.broadcasted_iota(jnp.int32, (16, 256), 1)
    in_row = (row >= 0) & (row < 64)
    first, last = lane == 0, lane == 255

    def inside(x):
        at = cell * 2 - 3 + x
        return in_row & jnp.broadcast_to((at >= 0) & (at < 64), (16, 256))

    def y_up(v):
        return pltpu.roll(v, 15, 0)

    def y_down(v):
        return pltpu.roll(v, 1, 0)

    def z_up(v):
        return jnp.where(last, 0.0, pltpu.roll(v, 255, 1))

    def z_down(v):
        return jnp.where(first, 0.0, pltpu.roll(v, 1, 1))

    def apply(u, lo, hi, keep):
        before = None
        for x in range(lo - 1, hi + 1):
            c = [u(k, x) for k in range(3)]
            u1y, u2z = y_up(c[1]), z_up(c[2])
            dv = (u(0, x + 1) - c[0]) + (u1y - c[1]) + (u2z - c[2])
            mask = inside(x)
            dv = jnp.where(mask, dv, 0.0)
            if x >= lo:
                ups = [(y_up(c[0]), z_up(c[0])), (u1y, z_up(c[1])), (y_up(c[2]), u2z)]
                grads = [before, y_down(dv), z_down(dv)]
                weight = sh[x] + 6.0 * MU
                for k in range(3):
                    beside = (u(k, x + 1) + u(k, x - 1)) + (ups[k][0] + y_down(c[k]))
                    beside = beside + (ups[k][1] + z_down(c[k]))
                    image = weight * c[k] - MU * beside + LAME * (grads[k] - dv)
                    keep(k, x, jnp.where(mask, image, 0.0))
            before = dv

    def put(ref):
        def keep(k, x, v):
            ref[k, x] = v

        return keep

    apply(lambda k, x: w0[k, x], 1, 6, put(w1))
    apply(lambda k, x: w1[k, x], 2, 5, put(w2))
    sums = [None] * 6

    def finish(k, x, v):
        w = [w0[k, x, 3:11, :], w1[k, x, 3:11, :], w2[k, x, 3:11, :], v[3:11, :]]
        for j in range(4):
            basis[j, k, x - 3] = w[j]
        for n, (i, j) in enumerate(((0, 0), (0, 1), (1, 1), (1, 2), (2, 2), (2, 3))):
            term = w[i] * w[j]
            sums[n] = term if sums[n] is None else sums[n] + term

    apply(lambda k, x: w2[k, x], 3, 4, finish)
    moments[...] = jnp.zeros((8, 128), F32)
    for n in range(6):
        line = jnp.sum(sums[n], axis=0, keepdims=True)
        moments[n : n + 1, :] = line[:, :128] + line[:, 128:]


def two_sum(a, b):
    s = a + b
    t = s - a
    return s, (a - (s - t)) + (b - t)


def two_product(a, b):
    def halves(v):
        t = 4097.0 * v
        high = t - (t - v)
        return high, v - high

    p = a * b
    ah, al = halves(a)
    bh, bl = halves(b)
    return p, ((ah * bh - p) + ah * bl + al * bh) + al * bl


def finish_kernel(parts, basis, mesh_adjoint, residual):
    sums = [(parts[n], None) for n in range(parts.shape[0])]
    while len(sums) > 1:
        pairs = []
        for (p, rest), (q, more_rest) in zip(sums[::2], sums[1::2]):
            high, low = two_sum(p, q)
            pairs.append((high, low if rest is None else low + (rest + more_rest)))
        sums = pairs
    high, low = sums[0]
    cut = 4096.0 * jnp.max(jnp.abs(high), axis=1, keepdims=True)
    lead = (high + cut) - cut
    rest = jnp.sum((high - lead) + low, axis=1, keepdims=True)
    high, low = two_sum(jnp.sum(lead, axis=1, keepdims=True), rest)
    high, low = jnp.broadcast_to(high, (8, 128)), jnp.broadcast_to(low, (8, 128))

    def line(v, n):
        return jnp.broadcast_to(v[n : n + 1, :], (8, 128))

    t = line(high, 1) / line(high, 0)
    centred = [line(high, 0) + line(low, 0)]
    for n in range(1, 6):
        product, error = two_product(t, high)
        error = error + t * low
        high, more = two_sum(pltpu.roll(high, 7, 0), -product)
        low = (pltpu.roll(low, 7, 0) - error) + more
        high, low = two_sum(high, low)
        centred.append(line(high, 0) + line(low, 0))

    def dot(u, v):
        total = None
        for i, p in enumerate(u):
            for j, q in enumerate(v):
                term = p * q * centred[i + j]
                total = term if total is None else total + term
        return total

    one = jnp.ones((8, 128), F32)
    r, p, x, now = [one], [one], [], centred[0]
    for sweep in range(ITERS):
        image = [t * p[0]] + [p[n - 1] + t * p[n] for n in range(1, len(p))] + [p[-1]]
        alpha = now / dot(p, image)
        x = [x[n] + alpha * p[n] if n < len(x) else alpha * p[n] for n in range(len(p))]
        r = [r[n] - alpha * image[n] if n < len(r) else -alpha * image[n] for n in range(len(image))]
        if sweep < ITERS - 1:
            new = dot(r, r)
            beta = new / now
            p = [r[n] + beta * p[n] if n < len(p) else r[n] for n in range(len(r))]
            now = new

    def monomials(c):
        out = [c[-1]]
        for term in c[-2::-1]:
            out = [term - t * out[0]] + [out[n - 1] - t * out[n] for n in range(1, len(out))] + [out[-1]]
        return [jnp.broadcast_to(v[0:1, 0:1], (8, 256)) for v in out]

    cx, cr = monomials(x), monomials(r)
    for k in range(3):
        for s in range(2):
            w = [basis[j, k, s] for j in range(4)]
            mesh_adjoint[k, s] = cx[0] * w[0] + cx[1] * w[1] + cx[2] * w[2]
            residual[k, s] = (cr[0] * w[0] + cr[1] * w[1]) + (cr[2] * w[2] + cr[3] * w[3])


def local(adjoint, flux_jac, shift):
    core = lax.axis_index("core")
    outer = lax.dynamic_index_in_dim(adjoint, core, 2, False)
    inner = lax.dynamic_index_in_dim(adjoint, 1 - core, 2, False)
    got_outer = send_pair(outer)
    got_inner = send_core(inner)

    six, nine, ten = (6, 8, 256), (9, 8, 256), (10, 8, 256)
    wide = [pltpu.VMEM((3, 72, 256), F32)]
    m0, m1, m2, m3 = call(
        sens_early_kernel, [nine, ten, ten, ten], (flux_jac, outer, got_inner, shift), wide
    )
    r2, r1, r3 = send_y(m2, 2), send_y(m1, 1), send_y(m3, 3)
    n0, n1, n2, n3 = call(sens_late_kernel, [nine] * 4, (flux_jac, inner, got_outer, m0), wide)
    q2, q1, q3 = send_y(n2, 2), send_y(n1, 1), send_y(n3, 3)
    own, out = call(sum_y_early_kernel, [six, (7, 8, 256)], (m0, r1, r3, r2, shift, n0))
    own, out = call(sum_y_late_kernel, [(12, 8, 256), (13, 8, 256)], (n0, q1, q3, q2, own, out))
    got = send_zh(out)
    sides = got[12].reshape(2, 4, 256)
    ends = [jnp.zeros((2, n, 256), F32) for n in (1, 3)]
    wider = jnp.concatenate([ends[0], sides[:, :2], shift, sides[:, 2:], ends[1]], axis=1)
    block = jnp.concatenate([(own + got[:12]).reshape(6, 16, 256), wider], axis=0)
    mate = send_core(block)
    far = send_pair(jnp.concatenate([block, mate[3:6]], axis=0))
    beyond = send_core(far[:3])

    scratch = pltpu.VMEM((3, 8, 16, 256), F32)
    basis, moments = call(
        krylov_kernel,
        [(4, 3, 2, 8, 256), (8, 128)],
        (block, mate, far, beyond),
        [scratch, scratch, scratch, pltpu.VMEM((8, 16, 256), F32)],
    )
    parts = lax.all_to_all(jnp.broadcast_to(moments, (16, 8, 128)), ("zh", "zl", "core"), 0, 0)
    moments = jnp.sum(parts, axis=0)
    parts = lax.all_to_all(jnp.broadcast_to(moments, (16, 8, 128)), ("y", "x"), 0, 0)
    shape = (3, 2, 8, 256)
    return tuple(call(finish_kernel, [shape, shape], (parts, basis)))


def solution(mesh):
    fine = Mesh(mesh.devices.reshape(SIZES), AXES)
    inst, cell = ("y", "zh"), ("x", "zl", "core")
    out = P(None, cell, inst, None)
    return jax.shard_map(
        local,
        mesh=fine,
        in_specs=(
            P(inst, None, cell, None, None),
            P(inst, None, None, cell, None, None),
            P(cell, inst, None),
        ),
        out_specs=(out, out),
        check_vma=False,
    )
```

```python
import jax
import jax.numpy as jnp
import numpy as np
from jax import lax
from jax.experimental import pallas as pl
from jax.experimental.pallas import tpu as pltpu
from jax.sharding import Mesh, PartitionSpec as P

ITERS = 3
MU = 1.0
LAME = 1.5
AXES = ("y", "zh", "x", "zl", "core")
SIZES = (4, 2, 4, 4, 2)
F32 = jnp.float32


def flat(at):
    index = 0
    for size, k in zip(SIZES, at):
        index = index * size + k
    return index


def send(v, move):
    pairs = []
    for at in np.ndindex(*SIZES):
        to = move(*at)
        if to is not None:
            pairs.append((flat(at), flat(to)))
    return lax.ppermute(v, AXES, pairs)


def send_y(v, d):
    return send(v, lambda y, zh, x, zl, core: ((y + d) % 4, zh, x, zl, core))


def send_zh(v):
    return send(v, lambda y, zh, x, zl, core: (y, 1 - zh, x, zl, core))


def send_core(v):
    return send(v, lambda y, zh, x, zl, core: (y, zh, x, zl, 1 - core))


def send_pair(v):
    def move(y, zh, x, zl, core):
        q = x * 4 + zl + (1 if core == 1 else -1)
        return (y, zh, q // 4, q % 4, 1 - core) if 0 <= q < 16 else None

    return send(v, move)


VMEM = pl.BlockSpec(memory_space=pltpu.VMEM)


def call(kernel, outs, args, scratch=()):
    return pl.pallas_call(
        kernel,
        out_shape=[jax.ShapeDtypeStruct(s, F32) for s in outs],
        in_specs=[VMEM] * len(args),
        out_specs=[VMEM] * len(outs),
        scratch_shapes=list(scratch),
        compiler_params=pltpu.CompilerParams(vmem_limit_bytes=24 * 1024 * 1024),
    )(*args)


def sens_of_slab(slab, sign, f, a, got, wide):
    zero = jnp.zeros((8, 256), F32)
    for k in range(3):
        wide[k, 0:8, :] = zero
        wide[k, 64:72, :] = zero
    for rows in range(0, 64, 16):
        span = slice(rows, rows + 16)
        total = [None] * 3
        for i in range(2):
            for v in range(5):
                step = got[i][v, span, :].astype(F32) - a[i, v, span, :].astype(F32)
                for k in range(3):
                    term = f[i, v, k, slab, span, :].astype(F32) * step
                    total[k] = term if total[k] is None else total[k] + term
        for k in range(3):
            wide[k, rows + 3 : rows + 19, :] = total[k] * sign


def cut(y, wide, outs):
    for d, out in enumerate(outs):
        first = pl.multiple_of(lax.rem(y + d, 4) * 16, 16)
        for k in range(3):
            out[k * 3 : k * 3 + 3] = wide[k, pl.ds(first, 24), :].reshape(3, 8, 256)


def sens_early_kernel(f, a, got0, got1, shift, m0, m1, m2, m3, wide):
    core = lax.axis_index("core")
    sens_of_slab(1 - core, jnp.where(core == 0, 1.0, -1.0), f, a, (got0, got1), wide)
    cut(lax.axis_index("y"), wide, (m0, m1, m2, m3))
    for out, span in ((m1, slice(6, 8)), (m2, slice(6, 8)), (m3, slice(0, 2))):
        for x in range(2):
            out[9, x * 2 : x * 2 + 2, :] = shift[x, span, :]
        out[9, 4:8, :] = jnp.zeros((4, 256), F32)


def sens_late_kernel(f, a, got, after, m0, m1, m2, m3, wide):
    core = lax.axis_index("core")
    sens_of_slab(core, jnp.where(core == 0, -1.0, 1.0), f, a, (got.at[0], got.at[1]), wide)
    cut(lax.axis_index("y"), wide, (m0, m1, m2, m3))


def sum_y(m0, r2, r1, r3, own, out):
    zh = lax.axis_index("zh")
    for s in range(3):
        for g in range(2):
            for half, to in ((zh, own), (1 - zh, out)):
                k = s * 3 + half + g
                to[s * 2 + g] = (m0[k] + r1[k]) + (r2[k] + r3[k])


def sum_y_early_kernel(m0, r1, r3, r2, shift, after, own, out):
    sum_y(m0, r2, r1, r3, own, out)
    low = lax.axis_index("zh") == 0
    for x in range(2):
        below = jnp.where(low, shift[x, 6:8, :], r1[9, x * 2 : x * 2 + 2, :])
        above = jnp.where(low, r3[9, x * 2 : x * 2 + 2, :], shift[x, 0:2, :])
        out[6, x * 4 : x * 4 + 2, :] = below
        out[6, x * 4 + 2 : x * 4 + 4, :] = above


def sum_y_late_kernel(m0, r1, r3, r2, own_early, out_early, own, out):
    sum_y(m0, r2, r1, r3, own, out)
    own[6:12] = own_early[...]
    out[6:13] = out_early[...]


def krylov_kernel(block, mate, far, beyond, basis, moments, w0, w1, w2, sh):
    core = lax.axis_index("core")
    inst = lax.axis_index("y") * 2 + lax.axis_index("zh")
    cell = lax.axis_index("x") * 8 + lax.axis_index("zl") * 2 + core

    def place(x):
        return x + core * (7 - 2 * x)

    for k in range(3):
        line = (
            far[8 + k], far[3 + k], far[k], block[k],
            block[3 + k], mate[3 + k], mate[k], beyond[k],
        )
        for x in range(8):
            w0[k, place(x)] = line[x]
    for x in range(2):
        sh[1 + core * 4 + x] = far[6 + x]
        sh[3 + x] = block[6 + x]
        sh[5 - core * 4 + x] = mate[6 + x]

    row = lax.broadcasted_iota(jnp.int32, (16, 256), 0) + (inst * 8 - 3)
    lane = lax.broadcasted_iota(jnp.int32, (16, 256), 1)
    in_row = (row >= 0) & (row < 64)
    first, last = lane == 0, lane == 255

    def inside(x):
        at = cell * 2 - 3 + x
        return in_row & jnp.broadcast_to((at >= 0) & (at < 64), (16, 256))

    def y_up(v):
        return pltpu.roll(v, 15, 0)

    def y_down(v):
        return pltpu.roll(v, 1, 0)

    def z_up(v):
        return jnp.where(last, 0.0, pltpu.roll(v, 255, 1))

    def z_down(v):
        return jnp.where(first, 0.0, pltpu.roll(v, 1, 1))

    def apply(u, lo, hi, keep):
        before = None
        for x in range(lo - 1, hi + 1):
            c = [u(k, x) for k in range(3)]
            u1y, u2z = y_up(c[1]), z_up(c[2])
            dv = (u(0, x + 1) - c[0]) + (u1y - c[1]) + (u2z - c[2])
            mask = inside(x)
            dv = jnp.where(mask, dv, 0.0)
            if x >= lo:
                ups = [(y_up(c[0]), z_up(c[0])), (u1y, z_up(c[1])), (y_up(c[2]), u2z)]
                grads = [before, y_down(dv), z_down(dv)]
                weight = sh[x] + 6.0 * MU
                for k in range(3):
                    beside = (u(k, x + 1) + u(k, x - 1)) + (ups[k][0] + y_down(c[k]))
                    beside = beside + (ups[k][1] + z_down(c[k]))
                    image = weight * c[k] - MU * beside + LAME * (grads[k] - dv)
                    keep(k, x, jnp.where(mask, image, 0.0))
            before = dv

    def put(ref):
        def keep(k, x, v):
            ref[k, x] = v

        return keep

    apply(lambda k, x: w0[k, x], 1, 6, put(w1))
    apply(lambda k, x: w1[k, x], 2, 5, put(w2))
    sums = [None] * 6

    def finish(k, x, v):
        w = [w0[k, x, 3:11, :], w1[k, x, 3:11, :], w2[k, x, 3:11, :], v[3:11, :]]
        for j in range(4):
            basis[j, k, x - 3] = w[j]
        for n, (i, j) in enumerate(((0, 0), (0, 1), (1, 1), (1, 2), (2, 2), (2, 3))):
            term = w[i] * w[j]
            sums[n] = term if sums[n] is None else sums[n] + term

    apply(lambda k, x: w2[k, x], 3, 4, finish)
    moments[...] = jnp.zeros((8, 128), F32)
    for n in range(6):
        line = jnp.sum(sums[n], axis=0, keepdims=True)
        moments[n : n + 1, :] = line[:, :128] + line[:, 128:]


def two_sum(a, b):
    s = a + b
    t = s - a
    return s, (a - (s - t)) + (b - t)


def two_product(a, b):
    def halves(v):
        t = 4097.0 * v
        high = t - (t - v)
        return high, v - high

    p = a * b
    ah, al = halves(a)
    bh, bl = halves(b)
    return p, ((ah * bh - p) + ah * bl + al * bh) + al * bl


def finish_kernel(parts, basis, mesh_adjoint, residual):
    sums = [(parts[n], None) for n in range(parts.shape[0])]
    while len(sums) > 1:
        pairs = []
        for (p, rest), (q, more_rest) in zip(sums[::2], sums[1::2]):
            high, low = two_sum(p, q)
            pairs.append((high, low if rest is None else low + (rest + more_rest)))
        sums = pairs
    high, low = sums[0]
    cut = 4096.0 * jnp.max(jnp.abs(high), axis=1, keepdims=True)
    lead = (high + cut) - cut
    rest = jnp.sum((high - lead) + low, axis=1, keepdims=True)
    high, low = two_sum(jnp.sum(lead, axis=1, keepdims=True), rest)
    high, low = jnp.broadcast_to(high, (8, 128)), jnp.broadcast_to(low, (8, 128))

    def line(v, n):
        return jnp.broadcast_to(v[n : n + 1, :], (8, 128))

    t = line(high, 1) / line(high, 0)
    centred = [line(high, 0) + line(low, 0)]
    for n in range(1, 6):
        product, error = two_product(t, high)
        error = error + t * low
        high, more = two_sum(pltpu.roll(high, 7, 0), -product)
        low = (pltpu.roll(low, 7, 0) - error) + more
        high, low = two_sum(high, low)
        centred.append(line(high, 0) + line(low, 0))

    def dot(u, v):
        total = None
        for i, p in enumerate(u):
            for j, q in enumerate(v):
                term = p * q * centred[i + j]
                total = term if total is None else total + term
        return total

    one = jnp.ones((8, 128), F32)
    r, p, x, now = [one], [one], [], centred[0]
    for sweep in range(ITERS):
        image = [t * p[0]] + [p[n - 1] + t * p[n] for n in range(1, len(p))] + [p[-1]]
        alpha = now / dot(p, image)
        x = [x[n] + alpha * p[n] if n < len(x) else alpha * p[n] for n in range(len(p))]
        r = [r[n] - alpha * image[n] if n < len(r) else -alpha * image[n] for n in range(len(image))]
        if sweep < ITERS - 1:
            new = dot(r, r)
            beta = new / now
            p = [r[n] + beta * p[n] if n < len(p) else r[n] for n in range(len(r))]
            now = new

    def monomials(c):
        out = [c[-1]]
        for term in c[-2::-1]:
            out = [term - t * out[0]] + [out[n - 1] - t * out[n] for n in range(1, len(out))] + [out[-1]]
        return [jnp.broadcast_to(v[0:1, 0:1], (8, 256)) for v in out]

    cx, cr = monomials(x), monomials(r)
    for k in range(3):
        for s in range(2):
            w = [basis[j, k, s] for j in range(4)]
            mesh_adjoint[k, s] = cx[0] * w[0] + cx[1] * w[1] + cx[2] * w[2]
            residual[k, s] = (cr[0] * w[0] + cr[1] * w[1]) + (cr[2] * w[2] + cr[3] * w[3])


def local(adjoint, flux_jac, shift):
    core = lax.axis_index("core")
    outer = lax.dynamic_index_in_dim(adjoint, core, 2, False)
    inner = lax.dynamic_index_in_dim(adjoint, 1 - core, 2, False)
    got_outer = send_pair(outer)
    got_inner = [send_core(inner[i]) for i in range(2)]

    six, nine, ten = (6, 8, 256), (9, 8, 256), (10, 8, 256)
    wide = [pltpu.VMEM((3, 72, 256), F32)]
    m0, m1, m2, m3 = call(
        sens_early_kernel, [nine, ten, ten, ten], (flux_jac, outer, *got_inner, shift), wide
    )
    r2, r1, r3 = send_y(m2, 2), send_y(m1, 1), send_y(m3, 3)
    n0, n1, n2, n3 = call(sens_late_kernel, [nine] * 4, (flux_jac, inner, got_outer, m0), wide)
    q2, q1, q3 = send_y(n2, 2), send_y(n1, 1), send_y(n3, 3)
    own, out = call(sum_y_early_kernel, [six, (7, 8, 256)], (m0, r1, r3, r2, shift, n0))
    own, out = call(sum_y_late_kernel, [(12, 8, 256), (13, 8, 256)], (n0, q1, q3, q2, own, out))
    got = send_zh(out)
    sides = got[12].reshape(2, 4, 256)
    ends = [jnp.zeros((2, n, 256), F32) for n in (1, 3)]
    wider = jnp.concatenate([ends[0], sides[:, :2], shift, sides[:, 2:], ends[1]], axis=1)
    block = jnp.concatenate([(own + got[:12]).reshape(6, 16, 256), wider], axis=0)
    mate = send_core(block)
    far = send_pair(jnp.concatenate([block, mate[3:6]], axis=0))
    beyond = send_core(far[:3])

    scratch = pltpu.VMEM((3, 8, 16, 256), F32)
    basis, moments = call(
        krylov_kernel,
        [(4, 3, 2, 8, 256), (8, 128)],
        (block, mate, far, beyond),
        [scratch, scratch, scratch, pltpu.VMEM((8, 16, 256), F32)],
    )
    parts = lax.all_to_all(jnp.broadcast_to(moments, (16, 8, 128)), ("zh", "zl", "core"), 0, 0)
    moments = jnp.sum(parts, axis=0)
    parts = lax.all_to_all(jnp.broadcast_to(moments, (16, 8, 128)), ("y", "x"), 0, 0)
    shape = (3, 2, 8, 256)
    return tuple(call(finish_kernel, [shape, shape], (parts, basis)))


def solution(mesh):
    fine = Mesh(mesh.devices.reshape(SIZES), AXES)
    inst, cell = ("y", "zh"), ("x", "zl", "core")
    out = P(None, cell, inst, None)
    return jax.shard_map(
        local,
        mesh=fine,
        in_specs=(
            P(inst, None, cell, None, None),
            P(inst, None, None, cell, None, None),
            P(cell, inst, None),
        ),
        out_specs=(out, out),
        check_vma=False,
    )
```

```python
import jax
import jax.numpy as jnp
import numpy as np
from jax import lax
from jax.experimental import pallas as pl
from jax.experimental.pallas import tpu as pltpu
from jax.sharding import Mesh, PartitionSpec as P

ITERS = 3
MU = 1.0
LAME = 1.5
AXES = ("y", "zh", "x", "zl", "core")
SIZES = (4, 2, 4, 4, 2)
F32 = jnp.float32


def flat(at):
    index = 0
    for size, k in zip(SIZES, at):
        index = index * size + k
    return index


def send(v, move):
    pairs = []
    for at in np.ndindex(*SIZES):
        to = move(*at)
        if to is not None:
            pairs.append((flat(at), flat(to)))
    return lax.ppermute(v, AXES, pairs)


def send_y(v, d):
    return send(v, lambda y, zh, x, zl, core: ((y + d) % 4, zh, x, zl, core))


def send_zh(v):
    return send(v, lambda y, zh, x, zl, core: (y, 1 - zh, x, zl, core))


def send_core(v):
    return send(v, lambda y, zh, x, zl, core: (y, zh, x, zl, 1 - core))


def send_pair(v):
    def move(y, zh, x, zl, core):
        q = x * 4 + zl + (1 if core == 1 else -1)
        return (y, zh, q // 4, q % 4, 1 - core) if 0 <= q < 16 else None

    return send(v, move)


VMEM = pl.BlockSpec(memory_space=pltpu.VMEM)


def call(kernel, outs, args, scratch=()):
    return pl.pallas_call(
        kernel,
        out_shape=[jax.ShapeDtypeStruct(s, F32) for s in outs],
        in_specs=[VMEM] * len(args),
        out_specs=[VMEM] * len(outs),
        scratch_shapes=list(scratch),
        compiler_params=pltpu.CompilerParams(vmem_limit_bytes=24 * 1024 * 1024),
    )(*args)


def sens_of_slab(slab, sign, f, a, got, wide):
    zero = jnp.zeros((8, 256), F32)
    for k in range(3):
        wide[k, 0:8, :] = zero
        wide[k, 64:72, :] = zero
    for rows in range(0, 64, 16):
        span = slice(rows, rows + 16)
        total = [None] * 3
        for i in range(2):
            for v in range(5):
                step = got[i][v, span, :].astype(F32) - a[i][v, span, :].astype(F32)
                for k in range(3):
                    term = f[i, v, k, slab, span, :].astype(F32) * step
                    total[k] = term if total[k] is None else total[k] + term
        for k in range(3):
            wide[k, rows + 3 : rows + 19, :] = total[k] * sign


def cut(y, wide, outs):
    for d, out in enumerate(outs):
        first = pl.multiple_of(lax.rem(y + d, 4) * 16, 16)
        for k in range(3):
            out[k * 3 : k * 3 + 3] = wide[k, pl.ds(first, 24), :].reshape(3, 8, 256)


def sens_early_kernel(f, a, got0, got1, shift, m0, m1, m2, m3, wide):
    core = lax.axis_index("core")
    sens_of_slab(1 - core, jnp.where(core == 0, 1.0, -1.0), f, (a.at[0], a.at[1]), (got0, got1), wide)
    cut(lax.axis_index("y"), wide, (m0, m1, m2, m3))
    for out, span in ((m1, slice(6, 8)), (m2, slice(6, 8)), (m3, slice(0, 2))):
        for x in range(2):
            out[9, x * 2 : x * 2 + 2, :] = shift[x, span, :]
        out[9, 4:8, :] = jnp.zeros((4, 256), F32)


def sens_late_kernel(f, a0, a1, got, after, m0, m1, m2, m3, wide):
    core = lax.axis_index("core")
    sens_of_slab(core, jnp.where(core == 0, -1.0, 1.0), f, (a0, a1), (got.at[0], got.at[1]), wide)
    cut(lax.axis_index("y"), wide, (m0, m1, m2, m3))


def sum_y(m0, r2, r1, r3, own, out):
    zh = lax.axis_index("zh")
    for s in range(3):
        for g in range(2):
            for half, to in ((zh, own), (1 - zh, out)):
                k = s * 3 + half + g
                to[s * 2 + g] = (m0[k] + r1[k]) + (r2[k] + r3[k])


def sum_y_early_kernel(m0, r1, r3, r2, shift, after, own, out):
    sum_y(m0, r2, r1, r3, own, out)
    low = lax.axis_index("zh") == 0
    for x in range(2):
        below = jnp.where(low, shift[x, 6:8, :], r1[9, x * 2 : x * 2 + 2, :])
        above = jnp.where(low, r3[9, x * 2 : x * 2 + 2, :], shift[x, 0:2, :])
        out[6, x * 4 : x * 4 + 2, :] = below
        out[6, x * 4 + 2 : x * 4 + 4, :] = above


def sum_y_late_kernel(m0, r1, r3, r2, own_early, out_early, own, out):
    sum_y(m0, r2, r1, r3, own, out)
    own[6:12] = own_early[...]
    out[6:13] = out_early[...]


def krylov_kernel(block, mate, far, beyond, basis, moments, w0, w1, w2, sh):
    core = lax.axis_index("core")
    inst = lax.axis_index("y") * 2 + lax.axis_index("zh")
    cell = lax.axis_index("x") * 8 + lax.axis_index("zl") * 2 + core

    def place(x):
        return x + core * (7 - 2 * x)

    for k in range(3):
        line = (
            far[8 + k], far[3 + k], far[k], block[k],
            block[3 + k], mate[3 + k], mate[k], beyond[k],
        )
        for x in range(8):
            w0[k, place(x)] = line[x]
    for x in range(2):
        sh[1 + core * 4 + x] = far[6 + x]
        sh[3 + x] = block[6 + x]
        sh[5 - core * 4 + x] = mate[6 + x]

    row = lax.broadcasted_iota(jnp.int32, (16, 256), 0) + (inst * 8 - 3)
    lane = lax.broadcasted_iota(jnp.int32, (16, 256), 1)
    in_row = (row >= 0) & (row < 64)
    first, last = lane == 0, lane == 255

    def inside(x):
        at = cell * 2 - 3 + x
        return in_row & jnp.broadcast_to((at >= 0) & (at < 64), (16, 256))

    def y_up(v):
        return pltpu.roll(v, 15, 0)

    def y_down(v):
        return pltpu.roll(v, 1, 0)

    def z_up(v):
        return jnp.where(last, 0.0, pltpu.roll(v, 255, 1))

    def z_down(v):
        return jnp.where(first, 0.0, pltpu.roll(v, 1, 1))

    def apply(u, lo, hi, keep):
        before = None
        for x in range(lo - 1, hi + 1):
            c = [u(k, x) for k in range(3)]
            u1y, u2z = y_up(c[1]), z_up(c[2])
            dv = (u(0, x + 1) - c[0]) + (u1y - c[1]) + (u2z - c[2])
            mask = inside(x)
            dv = jnp.where(mask, dv, 0.0)
            if x >= lo:
                ups = [(y_up(c[0]), z_up(c[0])), (u1y, z_up(c[1])), (y_up(c[2]), u2z)]
                grads = [before, y_down(dv), z_down(dv)]
                weight = sh[x] + 6.0 * MU
                for k in range(3):
                    beside = (u(k, x + 1) + u(k, x - 1)) + (ups[k][0] + y_down(c[k]))
                    beside = beside + (ups[k][1] + z_down(c[k]))
                    image = weight * c[k] - MU * beside + LAME * (grads[k] - dv)
                    keep(k, x, jnp.where(mask, image, 0.0))
            before = dv

    def put(ref):
        def keep(k, x, v):
            ref[k, x] = v

        return keep

    apply(lambda k, x: w0[k, x], 1, 6, put(w1))
    apply(lambda k, x: w1[k, x], 2, 5, put(w2))
    sums = [None] * 6

    def finish(k, x, v):
        w = [w0[k, x, 3:11, :], w1[k, x, 3:11, :], w2[k, x, 3:11, :], v[3:11, :]]
        for j in range(4):
            basis[j, k, x - 3] = w[j]
        for n, (i, j) in enumerate(((0, 0), (0, 1), (1, 1), (1, 2), (2, 2), (2, 3))):
            term = w[i] * w[j]
            sums[n] = term if sums[n] is None else sums[n] + term

    apply(lambda k, x: w2[k, x], 3, 4, finish)
    moments[...] = jnp.zeros((8, 128), F32)
    for n in range(6):
        line = jnp.sum(sums[n], axis=0, keepdims=True)
        moments[n : n + 1, :] = line[:, :128] + line[:, 128:]


def two_sum(a, b):
    s = a + b
    t = s - a
    return s, (a - (s - t)) + (b - t)


def two_product(a, b):
    def halves(v):
        t = 4097.0 * v
        high = t - (t - v)
        return high, v - high

    p = a * b
    ah, al = halves(a)
    bh, bl = halves(b)
    return p, ((ah * bh - p) + ah * bl + al * bh) + al * bl


def finish_kernel(parts, basis, mesh_adjoint, residual):
    sums = [(parts[n], None) for n in range(parts.shape[0])]
    while len(sums) > 1:
        pairs = []
        for (p, rest), (q, more_rest) in zip(sums[::2], sums[1::2]):
            high, low = two_sum(p, q)
            pairs.append((high, low if rest is None else low + (rest + more_rest)))
        sums = pairs
    high, low = sums[0]
    cut = 4096.0 * jnp.max(jnp.abs(high), axis=1, keepdims=True)
    lead = (high + cut) - cut
    rest = jnp.sum((high - lead) + low, axis=1, keepdims=True)
    high, low = two_sum(jnp.sum(lead, axis=1, keepdims=True), rest)
    high, low = jnp.broadcast_to(high, (8, 128)), jnp.broadcast_to(low, (8, 128))

    def line(v, n):
        return jnp.broadcast_to(v[n : n + 1, :], (8, 128))

    t = line(high, 1) / line(high, 0)
    centred = [line(high, 0) + line(low, 0)]
    for n in range(1, 6):
        product, error = two_product(t, high)
        error = error + t * low
        high, more = two_sum(pltpu.roll(high, 7, 0), -product)
        low = (pltpu.roll(low, 7, 0) - error) + more
        high, low = two_sum(high, low)
        centred.append(line(high, 0) + line(low, 0))

    def dot(u, v):
        total = None
        for i, p in enumerate(u):
            for j, q in enumerate(v):
                term = p * q * centred[i + j]
                total = term if total is None else total + term
        return total

    one = jnp.ones((8, 128), F32)
    r, p, x, now = [one], [one], [], centred[0]
    for sweep in range(ITERS):
        image = [t * p[0]] + [p[n - 1] + t * p[n] for n in range(1, len(p))] + [p[-1]]
        alpha = now / dot(p, image)
        x = [x[n] + alpha * p[n] if n < len(x) else alpha * p[n] for n in range(len(p))]
        r = [r[n] - alpha * image[n] if n < len(r) else -alpha * image[n] for n in range(len(image))]
        if sweep < ITERS - 1:
            new = dot(r, r)
            beta = new / now
            p = [r[n] + beta * p[n] if n < len(p) else r[n] for n in range(len(r))]
            now = new

    def monomials(c):
        out = [c[-1]]
        for term in c[-2::-1]:
            out = [term - t * out[0]] + [out[n - 1] - t * out[n] for n in range(1, len(out))] + [out[-1]]
        return [jnp.broadcast_to(v[0:1, 0:1], (8, 256)) for v in out]

    cx, cr = monomials(x), monomials(r)
    for k in range(3):
        for s in range(2):
            w = [basis[j, k, s] for j in range(4)]
            mesh_adjoint[k, s] = cx[0] * w[0] + cx[1] * w[1] + cx[2] * w[2]
            residual[k, s] = (cr[0] * w[0] + cr[1] * w[1]) + (cr[2] * w[2] + cr[3] * w[3])


def local(adjoint, flux_jac, shift):
    core = lax.axis_index("core")
    outer = lax.dynamic_index_in_dim(adjoint, core, 2, False)
    inner = [
        lax.dynamic_slice(adjoint, (i, 0, 1 - core, 0, 0), (1, 5, 1, 64, 256)).reshape(5, 64, 256)
        for i in range(2)
    ]
    got_outer = send_pair(outer)
    got_inner = [send_core(v) for v in inner]

    six, nine, ten = (6, 8, 256), (9, 8, 256), (10, 8, 256)
    wide = [pltpu.VMEM((3, 72, 256), F32)]
    m0, m1, m2, m3 = call(
        sens_early_kernel, [nine, ten, ten, ten], (flux_jac, outer, *got_inner, shift), wide
    )
    r2, r1, r3 = send_y(m2, 2), send_y(m1, 1), send_y(m3, 3)
    n0, n1, n2, n3 = call(sens_late_kernel, [nine] * 4, (flux_jac, *inner, got_outer, m0), wide)
    q2, q1, q3 = send_y(n2, 2), send_y(n1, 1), send_y(n3, 3)
    own, out = call(sum_y_early_kernel, [six, (7, 8, 256)], (m0, r1, r3, r2, shift, n0))
    own, out = call(sum_y_late_kernel, [(12, 8, 256), (13, 8, 256)], (n0, q1, q3, q2, own, out))
    got = send_zh(out)
    sides = got[12].reshape(2, 4, 256)
    ends = [jnp.zeros((2, n, 256), F32) for n in (1, 3)]
    wider = jnp.concatenate([ends[0], sides[:, :2], shift, sides[:, 2:], ends[1]], axis=1)
    block = jnp.concatenate([(own + got[:12]).reshape(6, 16, 256), wider], axis=0)
    mate = send_core(block)
    far = send_pair(jnp.concatenate([block, mate[3:6]], axis=0))
    beyond = send_core(far[:3])

    scratch = pltpu.VMEM((3, 8, 16, 256), F32)
    basis, moments = call(
        krylov_kernel,
        [(4, 3, 2, 8, 256), (8, 128)],
        (block, mate, far, beyond),
        [scratch, scratch, scratch, pltpu.VMEM((8, 16, 256), F32)],
    )
    parts = lax.all_to_all(jnp.broadcast_to(moments, (16, 8, 128)), ("zh", "zl", "core"), 0, 0)
    moments = jnp.sum(parts, axis=0)
    parts = lax.all_to_all(jnp.broadcast_to(moments, (16, 8, 128)), ("y", "x"), 0, 0)
    shape = (3, 2, 8, 256)
    return tuple(call(finish_kernel, [shape, shape], (parts, basis)))


def solution(mesh):
    fine = Mesh(mesh.devices.reshape(SIZES), AXES)
    inst, cell = ("y", "zh"), ("x", "zl", "core")
    out = P(None, cell, inst, None)
    return jax.shard_map(
        local,
        mesh=fine,
        in_specs=(
            P(inst, None, cell, None, None),
            P(inst, None, None, cell, None, None),
            P(cell, inst, None),
        ),
        out_specs=(out, out),
        check_vma=False,
    )
```
